32 devices in a mesh: band: 8 (over y, x, core), slab: 4 (over z).
Axes of the slice: x: 2, y: 2, z: 4, core: 2. Of those that a mesh axis runs over, the one named last changes fastest.
Arguments:
- wave_coeffs: float32 [16, 2, 128, 128, 128], P('band', None, 'slab'), may hold values from -12 to 12
- column_mask: int32 [128, 128], replicated, may hold values from 0 to 1, as said below
- occupations: float32 [16], P('band'), may hold values from 0.1 to 2
- core_density: float32 [128, 128, 128], P('band', 'slab'), may hold values from 0.05 to 0.5
Outputs:
- hartree: float32 [128, 128, 128], P('band', 'slab')
- xc_potential: float32 [128, 128, 128], P('band', 'slab')
The draws below stay inside these ranges and needn't reach their ends.
Inputs may be any that keep to these rules, and one draw needn't show every extreme that they name: `column_mask`: 1 marks a column of frequencies (first two indices) inside the cutoff; only columns whose shifted indices s1, s2 satisfy s1^2 + s2^2 <= 32^2 can be 1.
All inputs are finite; a program needn't handle non-finite values.
Results may differ from the reference program's by a relative error of at most 0.00035.
Values sent between devices are 32-bit elements; how exact they have to be, the bound alone decides.
A program may use at most 64 MiB of HBM per device.

```python
import math
import jax
import jax.numpy as jnp
from jax import lax

N = 128
BANDS = 16


def draw_column_mask(key, part):
    indices = jnp.arange(N, dtype=jnp.int32)
    shifted = (indices + N // 2) % N - N // 2
    squared = shifted[:, None] * shifted[:, None] + shifted[None, :] * shifted[None, :]
    radius = N // 4
    inside = squared <= radius * radius
    keeper = jax.random.randint(jax.random.fold_in(key, 17), (N, N), 0, 8) != 0
    return jnp.where(inside & keeper, 1, 0).astype(jnp.int32)


def shard_levels(rng, shape, shards, least, largest):
    loudness, own = 1.0, jax.random.fold_in(rng, 6)
    for dim, parts in shards:
        draws = jnp.exp(jax.random.uniform(jax.random.fold_in(own, dim), (parts,), jnp.float32, least / len(shards), largest / len(shards)))
        loudness = loudness * jnp.repeat(draws, shape[dim] // parts).reshape([-1 if axis == dim else 1 for axis in range(len(shape))])
    return loudness


def centred(own_key, dims, scale, most, cuts=(), kind=jnp.bfloat16):
    factor_of = shard_levels(own_key, dims, cuts, -0.22, 0.18) if cuts else 1.0
    values = jax.random.normal(own_key, dims, jnp.float32) * scale * factor_of
    return jnp.minimum(jnp.maximum(values, -most), most).astype(kind)


def setup_inputs(seed: int = 0) -> dict:
    arg_keys = jax.random.split(jax.random.key(seed), 5)
    wave_coeffs = centred(arg_keys[0], (BANDS, 2, N, N, N), 2.0, 12.0, ((0, 8), (2, 4)), jnp.float32)
    column_mask = draw_column_mask(jax.random.fold_in(arg_keys[4], 71), 0)
    occupations = jnp.clip(jnp.exp(math.log(2.0) - 2.9957323 * jax.random.uniform(arg_keys[2], (BANDS,), jnp.float32) ** shard_levels(arg_keys[2], (BANDS,), ((0, 8),), -0.2, 0.2)), 0.1, 2.0)
    core_density = jnp.clip(jnp.exp(math.log(0.5) - 2.3025851 * jax.random.uniform(arg_keys[3], (N, N, N), jnp.float32) ** shard_levels(arg_keys[3], (N, N, N), ((0, 8), (1, 4)), -0.2, 0.2)), 0.05, 0.5)
    return {"wave_coeffs": wave_coeffs, "column_mask": column_mask, "occupations": occupations, "core_density": core_density}


grid_spacing = 0.59
wigner_a = 0.44
wigner_b = 7.8


def kernel_block(extent, starts, amounts):
    pieces = []
    for offset, amount in zip(starts, amounts):
        frequency = offset + jnp.arange(amount, dtype=jnp.int32)
        shifted = (frequency + extent // 2) % extent - extent // 2
        pieces.append(shifted * shifted)
    squared = pieces[0][:, None, None] + pieces[1][None, :, None] + pieces[2][None, None, :]
    length = extent * grid_spacing
    scaled = (length * length / math.pi) / jnp.maximum(squared, 1).astype(jnp.float32)
    return jnp.where(squared == 0, 0.0, scaled)


def exchange_correlation(density):
    root_density = jnp.cbrt(density)
    radius = (3.0 / (4.0 * math.pi)) ** (1.0 / 3.0) / root_density
    exchange_part = -((3.0 / math.pi) ** (1.0 / 3.0)) * root_density
    shifted = radius + wigner_b
    correlation = -wigner_a / shifted - wigner_a * radius / (3.0 * shifted * shifted)
    return exchange_part + correlation


def reference(wave_coeffs, column_mask, occupations, core_density):
    inside = column_mask.astype(jnp.float32)[:, :, None]
    factor = float(N) ** 1.5

    def add_band(running, entries):
        coefficient, weight = entries
        wavefunction = jnp.fft.ifftn((coefficient[0] + 1j * coefficient[1]) * inside) * factor
        modulus = wavefunction.real * wavefunction.real + wavefunction.imag * wavefunction.imag
        return running + weight * modulus, None

    summed, _ = lax.scan(add_band, jnp.zeros((N, N, N), jnp.float32), (wave_coeffs, occupations))
    valence = summed / BANDS
    spectrum = jnp.fft.fftn(valence)
    hartree = jnp.fft.ifftn(spectrum * kernel_block(N, (0, 0, 0), (N, N, N))).real
    xc_potential = exchange_correlation(valence + core_density)
    return hartree, xc_potential
```

```python
import math

import jax
import jax.numpy as jnp
import ml_dtypes
import numpy as np
from jax import lax
from jax.experimental import pallas as pl
from jax.experimental.pallas import tpu as pltpu
from jax.sharding import PartitionSpec as P

grid_spacing = 0.59
wigner_a = 0.44
wigner_b = 7.8


def dft_tables(extent):
    indices = jnp.arange(extent, dtype=jnp.int32)
    phase = indices[:, None] * indices[None, :] % extent
    angle = phase.astype(jnp.float32) * (2.0 * math.pi / extent)
    return (jnp.cos(angle), jnp.sin(angle))


def kernel_block(extent, starts, amounts):
    pieces = []
    for offset, amount in zip(starts, amounts):
        frequency = offset + jnp.arange(amount, dtype=jnp.int32)
        shifted = (frequency + extent // 2) % extent - extent // 2
        pieces.append(shifted * shifted)
    squared = pieces[0][:, None, None] + pieces[1][None, :, None] + pieces[2][None, None, :]
    length = extent * grid_spacing
    scaled = length * length / math.pi / jnp.maximum(squared, 1).astype(jnp.float32)
    return jnp.where(squared == 0, 0.0, scaled)


def exchange_correlation(density):
    root_density = jnp.cbrt(density)
    radius = (3.0 / (4.0 * math.pi)) ** (1.0 / 3.0) / root_density
    exchange_part = -((3.0 / math.pi) ** (1.0 / 3.0)) * root_density
    shifted = radius + wigner_b
    correlation = -wigner_a / shifted - wigner_a * radius / (3.0 * shifted * shifted)
    return exchange_part + correlation


def project(pattern, values, matrix):
    return jnp.einsum(pattern, values, matrix, precision=lax.Precision.HIGHEST)


def rotate(real_part, imag_part, pattern, cosine_table, sine_table, direction):
    new_real = project(pattern, real_part, cosine_table) - direction * project(
        pattern, imag_part, sine_table
    )
    new_imag = direction * project(pattern, real_part, sine_table) + project(
        pattern, imag_part, cosine_table
    )
    return (new_real, new_imag)


def local(wave_coeffs, column_mask, occupations, core_density):
    local_bands = wave_coeffs.shape[0]
    row_count = wave_coeffs.shape[2]
    extent = wave_coeffs.shape[3]
    bands_all = lax.axis_size("band") * local_bands
    band_rows = extent // lax.axis_size("band")
    slab_index = lax.axis_index("slab")
    band_index = lax.axis_index("band")
    cosine_table, sine_table = dft_tables(extent)
    mask_rows = lax.dynamic_slice_in_dim(column_mask, slab_index * row_count, row_count, 0).astype(
        jnp.float32
    )
    masked = wave_coeffs * mask_rows[None, None, :, :, None]
    real_part, imag_part = rotate(
        masked[:, 0], masked[:, 1], "bxyz,zw->bxyw", cosine_table, sine_table, 1.0
    )
    real_part, imag_part = rotate(
        real_part, imag_part, "bxyz,yw->bxwz", cosine_table, sine_table, 1.0
    )
    stacked = jnp.stack((real_part, imag_part), axis=1)
    factor = 1.0 / (float(extent) ** 3 * bands_all)
    partial_value = jnp.zeros((extent, row_count, extent), jnp.float32)
    for member in range(local_bands):
        arrived = lax.all_to_all(stacked[member], "slab", split_axis=2, concat_axis=1, tiled=True)
        plane_real, plane_imag = rotate(
            arrived[0], arrived[1], "xyz,xw->wyz", cosine_table, sine_table, 1.0
        )
        partial_value = partial_value + occupations[member] * (
            plane_real * plane_real + plane_imag * plane_imag
        )
    partial_value = partial_value * factor
    density = lax.psum(partial_value, "band")
    own_density = lax.dynamic_slice_in_dim(density, band_index * band_rows, band_rows, 0)
    first_real = project("xyz,zw->xyw", density, cosine_table)
    first_imag = -project("xyz,zw->xyw", density, sine_table)
    line_real, line_imag = rotate(
        first_real, first_imag, "xyz,xw->wyz", cosine_table, sine_table, -1.0
    )
    arrived = lax.all_to_all(
        jnp.stack((line_real, line_imag)), "slab", split_axis=1, concat_axis=2, tiled=True
    )
    line_real, line_imag = rotate(
        arrived[0], arrived[1], "xyz,yw->xwz", cosine_table, sine_table, -1.0
    )
    kernel = kernel_block(extent, (slab_index * row_count, 0, 0), (row_count, extent, extent))
    line_real, line_imag = rotate(
        kernel * line_real, kernel * line_imag, "xyz,yw->xwz", cosine_table, sine_table, 1.0
    )
    arrived = lax.all_to_all(
        jnp.stack((line_real, line_imag)), "slab", split_axis=2, concat_axis=1, tiled=True
    )
    cosine_rows = lax.dynamic_slice_in_dim(cosine_table, band_index * band_rows, band_rows, 1)
    sine_rows = lax.dynamic_slice_in_dim(sine_table, band_index * band_rows, band_rows, 1)
    line_real, line_imag = rotate(
        arrived[0], arrived[1], "xyz,xw->wyz", cosine_rows, sine_rows, 1.0
    )
    spatial = project("xyz,zw->xyw", line_real, cosine_table) - project(
        "xyz,zw->xyw", line_imag, sine_table
    )
    hartree = spatial / float(extent) ** 3
    xc_potential = exchange_correlation(own_density + core_density)
    return (hartree, xc_potential)


def split(values):
    high = values.astype(jnp.bfloat16)
    low = (values - high.astype(jnp.float32)).astype(jnp.bfloat16)
    return high, low


def np_split(table):
    table = np.asarray(table, np.float32)
    high = table.astype(ml_dtypes.bfloat16)
    low = (table - high.astype(np.float32)).astype(ml_dtypes.bfloat16)
    return high, low


def np_phases(rows, columns, extent):
    angle = (np.outer(rows, columns) % extent) * (2.0 * np.pi / extent)
    return np.cos(angle), np.sin(angle)


def column_kernel(low_ref, high_ref, mask_ref, table_ref, out_ref):
    bands, _, rows = low_ref.shape[:3]
    for row in range(rows):
        parts = []
        for band in range(bands):
            pair = []
            for c in range(2):
                pair.append(
                    jnp.concatenate([low_ref[band, c, row], high_ref[band, c, row]], axis=0)
                )
            parts.append(pair)
        straight = jnp.concatenate([part for pair in parts for part in pair], axis=0)
        turned = jnp.concatenate([part for pair in parts for part in (-pair[1], pair[0])], axis=0)
        both = jnp.concatenate([straight, turned], axis=1)
        high, low = split(both)
        stacked = jnp.concatenate([high, low, high], axis=1)
        result = lax.dot_general(
            table_ref[...], stacked, (((1,), (1,)), ((), ())), preferred_element_type=jnp.float32
        )
        out_ref[:, row, :] = result * mask_ref[row : row + 1, :]


def transform_columns(wave_coeffs, lane_mask, extent):
    bands, _, rows = wave_coeffs.shape[:3]
    quarter = extent // 4
    lanes = bands * 2 * 2 * quarter
    indices = np.arange(extent)
    cosine, sine = np_phases(indices, indices, extent)
    high, low = np_split(np.concatenate([cosine, sine], axis=1))
    table = jnp.asarray(np.concatenate([high, high, low], axis=1))
    step = 8
    return pl.pallas_call(
        column_kernel,
        grid=(rows // step,),
        in_specs=[
            pl.BlockSpec((bands, 2, step, quarter, extent), lambda i: (0, 0, i, 0, 0)),
            pl.BlockSpec((bands, 2, step, quarter, extent), lambda i: (0, 0, i, 3, 0)),
            pl.BlockSpec((step, lanes), lambda i: (i, 0)),
            pl.BlockSpec((extent, 6 * extent), lambda i: (0, 0)),
        ],
        out_specs=pl.BlockSpec((extent, step, lanes), lambda i: (0, i, 0)),
        out_shape=jax.ShapeDtypeStruct((extent, rows, lanes), jnp.float32),
        compiler_params=pltpu.CompilerParams(vmem_limit_bytes=40 << 20),
        cost_estimate=pl.CostEstimate(
            flops=2 * rows * extent * lanes * 6 * extent,
            bytes_accessed=2 * 4 * extent * rows * lanes,
            transcendentals=0,
        ),
    )(wave_coeffs, wave_coeffs, lane_mask, table)


def plane_kernel(first_ref, last_ref, extra_ref, line_ref, weight_ref, left_ref, right_ref, out_ref):
    extent = out_ref.shape[-1]
    for plane in range(out_ref.shape[0]):
        rows = jnp.concatenate([first_ref[plane], last_ref[plane], extra_ref[plane]], axis=0)
        high, low = split(rows)
        turned = jnp.dot(
            left_ref[...],
            jnp.concatenate([high, low, high], axis=0),
            preferred_element_type=jnp.float32,
        )
        wide = jnp.concatenate([turned[:extent], turned[extent:]], axis=1)
        high, low = split(wide)
        psi = jnp.dot(
            jnp.concatenate([high, low, high], axis=1),
            right_ref[...],
            preferred_element_type=jnp.float32,
        )
        psi = psi + line_ref[plane]
        square = psi * psi * weight_ref[...]
        total = square[:, :extent]
        for part in range(1, square.shape[1] // extent):
            total = total + square[:, part * extent : (part + 1) * extent]
        out_ref[plane] = total


def plane_tables(bands, extent):
    quarter = extent // 4
    indices = np.arange(extent)
    kept = np.concatenate([np.arange(quarter), np.arange(3 * quarter, extent)])
    count = 2 * quarter
    cosine, sine = np_phases(indices, np.concatenate([kept, [quarter]]), extent)
    left = np.zeros((2 * extent, count + 16))
    left[:extent, : count + 1] = cosine
    left[extent:, : count + 1] = sine
    high, low = np_split(left)
    left = np.concatenate([high, high, low], axis=1)
    cosine, sine = np_phases(kept, indices, extent)
    lanes = bands * 2 * count
    right = np.zeros((2, bands, 2, count, bands, 2, extent))
    for band in range(bands):
        right[0, band, 0, :, band, 0] = cosine
        right[0, band, 1, :, band, 0] = -sine
        right[1, band, 0, :, band, 0] = -sine
        right[1, band, 1, :, band, 0] = -cosine
        right[0, band, 0, :, band, 1] = sine
        right[0, band, 1, :, band, 1] = cosine
        right[1, band, 0, :, band, 1] = cosine
        right[1, band, 1, :, band, 1] = -sine
    high, low = np_split(right.reshape(2 * lanes, bands * 2 * extent))
    right = np.concatenate([high, high, low], axis=0)
    return jnp.asarray(left), jnp.asarray(right)


def partial_density(first, last, extra, line, weight, extent):
    planes, rows, lanes = first.shape
    bands = line.shape[2] // (2 * extent)
    left, right = plane_tables(bands, extent)
    step = 4
    return pl.pallas_call(
        plane_kernel,
        grid=(planes // step,),
        in_specs=[
            pl.BlockSpec((step, rows, lanes), lambda i: (i, 0, 0)),
            pl.BlockSpec((step, rows, lanes), lambda i: (i, 0, 0)),
            pl.BlockSpec((step, 16, lanes), lambda i: (i, 0, 0)),
            pl.BlockSpec((step, 1, line.shape[2]), lambda i: (i, 0, 0)),
            pl.BlockSpec((1, line.shape[2]), lambda i: (0, 0)),
            pl.BlockSpec(left.shape, lambda i: (0, 0)),
            pl.BlockSpec(right.shape, lambda i: (0, 0)),
        ],
        out_specs=pl.BlockSpec((step, extent, extent), lambda i: (i, 0, 0)),
        out_shape=jax.ShapeDtypeStruct((planes, extent, extent), jnp.float32),
        compiler_params=pltpu.CompilerParams(vmem_limit_bytes=40 << 20),
        cost_estimate=pl.CostEstimate(
            flops=2 * planes * extent * right.shape[0] * right.shape[1],
            bytes_accessed=4 * planes * (2 * rows * lanes + extent * extent),
            transcendentals=0,
        ),
    )(first, last, extra, line, weight, left, right)


def exchange(columns, slab_index, planes):
    def chunk(index):
        return lax.dynamic_slice_in_dim(columns, index * planes, planes, 0)

    low_end = slab_index < 2
    far = lax.ppermute(chunk(jnp.where(low_end, 3, 0)), "slab", [(0, 3), (3, 0)])
    near = lax.ppermute(chunk(jnp.where(low_end, 1, 2)), "slab", [(0, 1), (3, 2)])
    middle = lax.ppermute(chunk(jnp.where(low_end, 2, 1)), "slab", [(0, 2), (3, 1)])
    own = chunk(slab_index)
    first = lax.select_n(slab_index, own, near, middle, far)
    last = lax.select_n(slab_index, far, middle, near, own)
    return first, last


def potential(density, extent, kernel_axes):
    size = lax.axis_size(kernel_axes)
    member = lax.axis_index(kernel_axes)
    band_count, slab_count = lax.axis_size("band"), lax.axis_size("slab")
    rows, columns = density.shape[:2]
    half = extent // 2 + 1
    each = -(-half // size)
    frequencies = np.arange(each * size)
    cosine, sine = np_phases(frequencies, np.arange(extent), extent)
    inside = (frequencies < half)[:, None]
    table = np.stack([cosine * inside, -sine * inside]).reshape(2, size, each, extent)
    forward = table.transpose(1, 0, 2, 3).reshape(-1, extent)
    weights = np.where((frequencies == 0) | (frequencies == extent // 2), 1.0, 2.0)
    backward = forward * np.tile(weights.reshape(size, 1, each), (1, 2, 1)).reshape(-1, 1)
    backward = backward / float(extent) ** 3
    forward = jnp.asarray(forward, jnp.float32)
    backward = jnp.asarray(backward, jnp.float32)
    lines = project("kz,pz->kp", forward, density.reshape(rows * columns, extent))
    planes = lax.all_to_all(lines, kernel_axes, split_axis=0, concat_axis=0, tiled=True)
    planes = planes.reshape(band_count, slab_count, 2 * each, rows, columns)
    planes = planes.transpose(2, 0, 3, 1, 4).reshape(2, each, extent, extent)
    cosine_table, sine_table = dft_tables(extent)
    real_part, imag_part = planes[0], planes[1]
    real_part, imag_part = rotate(real_part, imag_part, "kxy,yw->kxw", cosine_table, sine_table, -1.0)
    real_part, imag_part = rotate(real_part, imag_part, "kxy,xw->kwy", cosine_table, sine_table, -1.0)
    kernel = kernel_block(extent, (member * each, 0, 0), (each, extent, extent))
    real_part, imag_part = kernel * real_part, kernel * imag_part
    real_part, imag_part = rotate(real_part, imag_part, "kxy,xw->kwy", cosine_table, sine_table, 1.0)
    real_part, imag_part = rotate(real_part, imag_part, "kxy,yw->kxw", cosine_table, sine_table, 1.0)
    planes = jnp.stack((real_part, imag_part)).reshape(
        2 * each, band_count, rows, slab_count, columns
    )
    planes = planes.transpose(1, 3, 0, 2, 4).reshape(-1, rows * columns)
    lines = lax.all_to_all(planes, kernel_axes, split_axis=0, concat_axis=0, tiled=True)
    return project("kp,kz->pz", lines, backward).reshape(rows, columns, extent)


def quartered(wave_coeffs, column_mask, occupations, core_density):
    bands, _, rows, extent = wave_coeffs.shape[:4]
    quarter = extent // 4
    slab_index = lax.axis_index("slab")
    mask_rows = lax.dynamic_slice_in_dim(column_mask, slab_index * rows, rows, 0).astype(jnp.float32)
    kept = jnp.concatenate([mask_rows[:, :quarter], mask_rows[:, 3 * quarter :]], axis=1)
    lane_mask = jnp.tile(kept, (1, 2 * bands))
    columns = transform_columns(wave_coeffs, lane_mask, extent)
    first, last = exchange(columns, slab_index, rows)

    cosine_table, sine_table = dft_tables(extent)
    single = jnp.stack((wave_coeffs[:, :, 0, quarter], wave_coeffs[:, :, 0, 0]))
    single = single * jnp.stack(
        (
            jnp.where(slab_index == 0, column_mask[0, quarter], 0),
            jnp.where(slab_index == 1, column_mask[quarter, 0], 0),
        )
    ).astype(jnp.float32)[:, None, None, None]
    single = lax.psum(single, "slab")
    cosine_part = lax.dynamic_slice_in_dim(cosine_table, slab_index * rows, rows, 0)
    sine_part = lax.dynamic_slice_in_dim(sine_table, slab_index * rows, rows, 0)
    single_real, single_imag = rotate(
        single[:, :, 0], single[:, :, 1], "kbz,wz->kbw", cosine_part, sine_part, 1.0
    )
    phase_real, phase_imag = cosine_table[quarter], sine_table[quarter]
    line_real = single_real[0, ..., None] * phase_real - single_imag[0, ..., None] * phase_imag
    line_imag = single_real[0, ..., None] * phase_imag + single_imag[0, ..., None] * phase_real
    line = jnp.stack((line_real, line_imag), axis=1).transpose(2, 0, 1, 3)
    line = line.reshape(rows, 1, bands * 2 * extent)
    spot = jnp.stack((single_real[1], single_imag[1]), axis=1).transpose(2, 0, 1)
    extra = jnp.pad(spot[:, None, :, :, None], ((0, 0), (0, 15), (0, 0), (0, 0), (0, 2 * quarter - 1)))
    extra = extra.reshape(rows, 16, bands * 4 * quarter)
    bands_all = lax.axis_size("band") * bands
    weight = jnp.repeat(occupations / (float(extent) ** 3 * bands_all), 2 * extent)[None]
    partial = partial_density(first, last, extra, line, weight, extent)
    summed = lax.psum_scatter(partial, "band", scatter_dimension=1, tiled=True)
    turned = summed.transpose(2, 0, 1)
    turned = lax.all_to_all(turned, "slab", split_axis=0, concat_axis=1, tiled=True)
    density = turned.transpose(2, 0, 1)
    xc_potential = exchange_correlation(density + core_density)
    hartree = potential(density, extent, ("band", "slab"))
    return (hartree, xc_potential)


def solution(mesh):
    body = quartered if mesh.shape["slab"] == 4 else local
    return jax.shard_map(
        body,
        mesh=mesh,
        in_specs=(P("band", None, "slab", None, None), P(), P("band"), P("band", "slab", None)),
        out_specs=(P("band", "slab", None), P("band", "slab", None)),
        check_vma=False,
    )
```

```python
import math

import jax
import jax.numpy as jnp
import ml_dtypes
import numpy as np
from jax import lax
from jax.experimental import pallas as pl
from jax.experimental.pallas import tpu as pltpu
from jax.sharding import PartitionSpec as P

grid_spacing = 0.59
wigner_a = 0.44
wigner_b = 7.8


def dft_tables(extent):
    indices = jnp.arange(extent, dtype=jnp.int32)
    phase = indices[:, None] * indices[None, :] % extent
    angle = phase.astype(jnp.float32) * (2.0 * math.pi / extent)
    return (jnp.cos(angle), jnp.sin(angle))


def kernel_block(extent, starts, amounts):
    pieces = []
    for offset, amount in zip(starts, amounts):
        frequency = offset + jnp.arange(amount, dtype=jnp.int32)
        shifted = (frequency + extent // 2) % extent - extent // 2
        pieces.append(shifted * shifted)
    squared = pieces[0][:, None, None] + pieces[1][None, :, None] + pieces[2][None, None, :]
    length = extent * grid_spacing
    scaled = length * length / math.pi / jnp.maximum(squared, 1).astype(jnp.float32)
    return jnp.where(squared == 0, 0.0, scaled)


def exchange_correlation(density):
    root_density = jnp.cbrt(density)
    radius = (3.0 / (4.0 * math.pi)) ** (1.0 / 3.0) / root_density
    exchange_part = -((3.0 / math.pi) ** (1.0 / 3.0)) * root_density
    shifted = radius + wigner_b
    correlation = -wigner_a / shifted - wigner_a * radius / (3.0 * shifted * shifted)
    return exchange_part + correlation


def project(pattern, values, matrix):
    return jnp.einsum(pattern, values, matrix, precision=lax.Precision.HIGHEST)


def rotate(real_part, imag_part, pattern, cosine_table, sine_table, direction):
    new_real = project(pattern, real_part, cosine_table) - direction * project(
        pattern, imag_part, sine_table
    )
    new_imag = direction * project(pattern, real_part, sine_table) + project(
        pattern, imag_part, cosine_table
    )
    return (new_real, new_imag)


def local(wave_coeffs, column_mask, occupations, core_density):
    local_bands = wave_coeffs.shape[0]
    row_count = wave_coeffs.shape[2]
    extent = wave_coeffs.shape[3]
    bands_all = lax.axis_size("band") * local_bands
    band_rows = extent // lax.axis_size("band")
    slab_index = lax.axis_index("slab")
    band_index = lax.axis_index("band")
    cosine_table, sine_table = dft_tables(extent)
    mask_rows = lax.dynamic_slice_in_dim(column_mask, slab_index * row_count, row_count, 0).astype(
        jnp.float32
    )
    masked = wave_coeffs * mask_rows[None, None, :, :, None]
    real_part, imag_part = rotate(
        masked[:, 0], masked[:, 1], "bxyz,zw->bxyw", cosine_table, sine_table, 1.0
    )
    real_part, imag_part = rotate(
        real_part, imag_part, "bxyz,yw->bxwz", cosine_table, sine_table, 1.0
    )
    stacked = jnp.stack((real_part, imag_part), axis=1)
    factor = 1.0 / (float(extent) ** 3 * bands_all)
    partial_value = jnp.zeros((extent, row_count, extent), jnp.float32)
    for member in range(local_bands):
        arrived = lax.all_to_all(stacked[member], "slab", split_axis=2, concat_axis=1, tiled=True)
        plane_real, plane_imag = rotate(
            arrived[0], arrived[1], "xyz,xw->wyz", cosine_table, sine_table, 1.0
        )
        partial_value = partial_value + occupations[member] * (
            plane_real * plane_real + plane_imag * plane_imag
        )
    partial_value = partial_value * factor
    density = lax.psum(partial_value, "band")
    own_density = lax.dynamic_slice_in_dim(density, band_index * band_rows, band_rows, 0)
    first_real = project("xyz,zw->xyw", density, cosine_table)
    first_imag = -project("xyz,zw->xyw", density, sine_table)
    line_real, line_imag = rotate(
        first_real, first_imag, "xyz,xw->wyz", cosine_table, sine_table, -1.0
    )
    arrived = lax.all_to_all(
        jnp.stack((line_real, line_imag)), "slab", split_axis=1, concat_axis=2, tiled=True
    )
    line_real, line_imag = rotate(
        arrived[0], arrived[1], "xyz,yw->xwz", cosine_table, sine_table, -1.0
    )
    kernel = kernel_block(extent, (slab_index * row_count, 0, 0), (row_count, extent, extent))
    line_real, line_imag = rotate(
        kernel * line_real, kernel * line_imag, "xyz,yw->xwz", cosine_table, sine_table, 1.0
    )
    arrived = lax.all_to_all(
        jnp.stack((line_real, line_imag)), "slab", split_axis=2, concat_axis=1, tiled=True
    )
    cosine_rows = lax.dynamic_slice_in_dim(cosine_table, band_index * band_rows, band_rows, 1)
    sine_rows = lax.dynamic_slice_in_dim(sine_table, band_index * band_rows, band_rows, 1)
    line_real, line_imag = rotate(
        arrived[0], arrived[1], "xyz,xw->wyz", cosine_rows, sine_rows, 1.0
    )
    spatial = project("xyz,zw->xyw", line_real, cosine_table) - project(
        "xyz,zw->xyw", line_imag, sine_table
    )
    hartree = spatial / float(extent) ** 3
    xc_potential = exchange_correlation(own_density + core_density)
    return (hartree, xc_potential)


def split(values):
    high = values.astype(jnp.bfloat16)
    low = (values - high.astype(jnp.float32)).astype(jnp.bfloat16)
    return high, low


def np_split(table):
    table = np.asarray(table, np.float32)
    high = table.astype(ml_dtypes.bfloat16)
    low = (table - high.astype(np.float32)).astype(ml_dtypes.bfloat16)
    return high, low


def np_phases(rows, columns, extent):
    angle = (np.outer(rows, columns) % extent) * (2.0 * np.pi / extent)
    return np.cos(angle), np.sin(angle)


def column_kernel(low_ref, high_ref, mask_ref, table_ref, out_ref):
    bands, _, rows = low_ref.shape[:3]
    for row in range(rows):
        parts = []
        for band in range(bands):
            pair = []
            for c in range(2):
                pair.append(
                    jnp.concatenate([low_ref[band, c, row], high_ref[band, c, row]], axis=0)
                )
            parts.append(pair)
        straight = jnp.concatenate([part for pair in parts for part in pair], axis=0)
        turned = jnp.concatenate([part for pair in parts for part in (-pair[1], pair[0])], axis=0)
        both = jnp.concatenate([straight, turned], axis=1)
        high, low = split(both)
        stacked = jnp.concatenate([high, low, high], axis=1)
        result = lax.dot_general(
            table_ref[...], stacked, (((1,), (1,)), ((), ())), preferred_element_type=jnp.float32
        )
        out_ref[:, row, :] = result * mask_ref[row : row + 1, :]


def transform_columns(wave_coeffs, lane_mask, extent):
    bands, _, rows = wave_coeffs.shape[:3]
    quarter = extent // 4
    lanes = bands * 2 * 2 * quarter
    indices = np.arange(extent)
    cosine, sine = np_phases(indices, indices, extent)
    high, low = np_split(np.concatenate([cosine, sine], axis=1))
    table = jnp.asarray(np.concatenate([high, high, low], axis=1))
    step = 8
    return pl.pallas_call(
        column_kernel,
        grid=(rows // step,),
        in_specs=[
            pl.BlockSpec((bands, 2, step, quarter, extent), lambda i: (0, 0, i, 0, 0)),
            pl.BlockSpec((bands, 2, step, quarter, extent), lambda i: (0, 0, i, 3, 0)),
            pl.BlockSpec((step, lanes), lambda i: (i, 0)),
            pl.BlockSpec((extent, 6 * extent), lambda i: (0, 0)),
        ],
        out_specs=pl.BlockSpec((extent, step, lanes), lambda i: (0, i, 0)),
        out_shape=jax.ShapeDtypeStruct((extent, rows, lanes), jnp.float32),
        compiler_params=pltpu.CompilerParams(vmem_limit_bytes=40 << 20),
        cost_estimate=pl.CostEstimate(
            flops=2 * rows * extent * lanes * 6 * extent,
            bytes_accessed=2 * 4 * extent * rows * lanes,
            transcendentals=0,
        ),
    )(wave_coeffs, wave_coeffs, lane_mask, table)


def density_kernel(
    columns_ref,
    lines_ref,
    weight_ref,
    left_ref,
    right_ref,
    out_ref,
    land,
    extra,
    line,
    partial,
    shares,
    column_send,
    column_recv,
    small_send,
    small_recv,
    local_sem,
    share_send,
    share_recv,
):
    mesh_ids = pl.DeviceIdType.MESH
    planes, rows, extent = out_ref.shape
    peers = extent // rows
    pieces = column_recv.shape[1]
    step = planes // pieces
    band, slab = lax.axis_index("band"), lax.axis_index("slab")

    barrier = pltpu.get_barrier_semaphore()
    for shift in range(1, peers):
        pl.semaphore_signal(
            barrier, inc=1, device_id=((band + shift) % peers, slab), device_id_type=mesh_ids
        )
    for shift in range(1, 4):
        pl.semaphore_signal(
            barrier, inc=1, device_id=(band, (slab + shift) % 4), device_id_type=mesh_ids
        )
    pl.semaphore_wait(barrier, peers - 1 + 3)

    def column_copy(side, order, target, piece):
        return pltpu.make_async_remote_copy(
            src_ref=columns_ref.at[pl.ds(target * planes + piece * step, step)],
            dst_ref=land.at[side, pl.ds(piece * step, step)],
            send_sem=column_send.at[order, piece],
            recv_sem=column_recv.at[side, piece],
            device_id=(band, target),
            device_id_type=mesh_ids,
        )

    def line_copy(order, target):
        return pltpu.make_async_remote_copy(
            src_ref=lines_ref.at[pl.ds(target * planes, planes)],
            dst_ref=line,
            send_sem=small_send.at[order],
            recv_sem=small_recv.at[0],
            device_id=(band, target),
            device_id_type=mesh_ids,
        )

    def extra_copy(order, target):
        return pltpu.make_async_remote_copy(
            src_ref=columns_ref.at[pl.ds(target * planes, planes), pl.ds(0, 8)],
            dst_ref=extra,
            send_sem=small_send.at[order],
            recv_sem=small_recv.at[1],
            device_id=(band, target),
            device_id_type=mesh_ids,
        )

    def own_columns(side, slab_number):
        return pltpu.make_async_copy(
            columns_ref.at[pl.ds(slab_number * planes, planes)], land.at[side], local_sem.at[0]
        )

    def own_line():
        return pltpu.make_async_copy(lines_ref.at[pl.ds(0, planes)], line, local_sem.at[1])

    def own_extra():
        return pltpu.make_async_copy(
            columns_ref.at[pl.ds(planes, planes), pl.ds(0, 8)], extra, local_sem.at[1]
        )

    ends = ((0, 0, (3, 2, 1)), (1, 3, (0, 1, 2)))

    @pl.when(slab == 0)
    def _():
        for order, target in enumerate((3, 2, 1)):
            line_copy(order, target).start()
        own_line().start()

    @pl.when(slab == 1)
    def _():
        for order, target in enumerate((0, 2, 3)):
            extra_copy(order, target).start()
        own_extra().start()

    for side, number, targets in ends:

        @pl.when(slab == number)
        def _():
            for piece in range(pieces):
                for order, target in enumerate(targets):
                    column_copy(side, order, target, piece).start()
            own_columns(side, number).start()

    @pl.when(slab == 0)
    def _():
        own_line().wait()
        own_columns(0, 0).wait()

    @pl.when(slab != 0)
    def _():
        line_copy(0, 1).wait_recv()

    @pl.when(slab == 1)
    def _():
        own_extra().wait()

    @pl.when(slab != 1)
    def _():
        extra_copy(0, 2).wait_recv()

    @pl.when(slab == 3)
    def _():
        own_columns(1, 3).wait()

    def share_copy(shift, piece):
        peer = (band + shift) % peers
        return pltpu.make_async_remote_copy(
            src_ref=partial.at[
                pl.ds(piece * step, step), pl.ds(pl.multiple_of(peer * rows, rows), rows)
            ],
            dst_ref=shares.at[shift - 1, pl.ds(piece * step, step)],
            send_sem=share_send.at[shift - 1, piece],
            recv_sem=share_recv.at[shift - 1, piece],
            device_id=(peer, slab),
            device_id_type=mesh_ids,
        )

    def transform(plane, carry):
        filler = jnp.zeros((8, land.shape[3]), jnp.float32)
        values = jnp.concatenate([land[0, plane], land[1, plane], extra[plane], filler], axis=0)
        high, low = split(values)
        turned = jnp.dot(
            left_ref[...],
            jnp.concatenate([high, low, high], axis=0),
            preferred_element_type=jnp.float32,
        )
        wide = jnp.concatenate([turned[:extent], turned[extent:]], axis=1)
        high, low = split(wide)
        psi = jnp.dot(
            jnp.concatenate([high, low, high], axis=1),
            right_ref[...],
            preferred_element_type=jnp.float32,
        )
        psi = psi + line[pl.ds(plane, 1), :]
        square = psi * psi * weight_ref[...]
        total = square[:, :extent]
        for part in range(1, square.shape[1] // extent):
            total = total + square[:, part * extent : (part + 1) * extent]
        partial[plane] = total
        return carry

    for piece in range(pieces):

        @pl.when(slab != 0)
        def _():
            column_copy(0, 0, 1, piece).wait_recv()

        @pl.when(slab != 3)
        def _():
            column_copy(1, 0, 1, piece).wait_recv()

        lax.fori_loop(piece * step, (piece + 1) * step, transform, 0)
        for shift in range(1, peers):
            share_copy(shift, piece).start()

    for piece in range(pieces):
        section = pl.ds(piece * step, step)
        own = pl.ds(pl.multiple_of(band * rows, rows), rows)
        total = partial[section, own, :]
        for shift in range(1, peers):
            share_copy(shift, piece).wait_recv()
            total = total + shares[shift - 1, section]
        out_ref[section] = total

    for piece in range(pieces):
        for shift in range(1, peers):
            share_copy(shift, piece).wait_send()
    for side, number, targets in ends:

        @pl.when(slab == number)
        def _():
            for piece in range(pieces):
                for order, target in enumerate(targets):
                    column_copy(side, order, target, piece).wait_send()

    @pl.when(slab == 0)
    def _():
        for order, target in enumerate((3, 2, 1)):
            line_copy(order, target).wait_send()

    @pl.when(slab == 1)
    def _():
        for order, target in enumerate((0, 2, 3)):
            extra_copy(order, target).wait_send()


def plane_tables(bands, extent):
    quarter = extent // 4
    indices = np.arange(extent)
    kept = np.concatenate([np.arange(quarter), np.arange(3 * quarter, extent)])
    count = 2 * quarter
    cosine, sine = np_phases(indices, np.concatenate([kept, [quarter]]), extent)
    left = np.zeros((2 * extent, count + 16))
    left[:extent, : count + 1] = cosine
    left[extent:, : count + 1] = sine
    high, low = np_split(left)
    left = np.concatenate([high, high, low], axis=1)
    cosine, sine = np_phases(kept, indices, extent)
    lanes = bands * 2 * count
    right = np.zeros((2, bands, 2, count, bands, 2, extent))
    for band in range(bands):
        right[0, band, 0, :, band, 0] = cosine
        right[0, band, 1, :, band, 0] = -sine
        right[1, band, 0, :, band, 0] = -sine
        right[1, band, 1, :, band, 0] = -cosine
        right[0, band, 0, :, band, 1] = sine
        right[0, band, 1, :, band, 1] = cosine
        right[1, band, 0, :, band, 1] = cosine
        right[1, band, 1, :, band, 1] = -sine
    high, low = np_split(right.reshape(2 * lanes, bands * 2 * extent))
    right = np.concatenate([high, high, low], axis=0)
    return jnp.asarray(left), jnp.asarray(right)


def summed_density(columns, lines, weight, extent):
    _, rows, lanes = columns.shape
    bands = lines.shape[1] // (2 * extent)
    planes = extent // 4
    peers = lax.axis_size("band")
    share = extent // peers
    left, right = plane_tables(bands, extent)
    pieces = 4
    vmem = pl.BlockSpec(memory_space=pltpu.VMEM)
    return pl.pallas_call(
        density_kernel,
        in_specs=[pl.BlockSpec(memory_space=pl.ANY), vmem, vmem, vmem, vmem],
        out_specs=vmem,
        out_shape=jax.ShapeDtypeStruct((planes, share, extent), jnp.float32),
        scratch_shapes=[
            pltpu.VMEM((2, planes, rows, lanes), jnp.float32),
            pltpu.VMEM((planes, 8, lanes), jnp.float32),
            pltpu.VMEM((planes, lines.shape[1]), jnp.float32),
            pltpu.VMEM((planes, extent, extent), jnp.float32),
            pltpu.VMEM((peers - 1, planes, share, extent), jnp.float32),
            pltpu.SemaphoreType.DMA((3, pieces)),
            pltpu.SemaphoreType.DMA((2, pieces)),
            pltpu.SemaphoreType.DMA((3,)),
            pltpu.SemaphoreType.DMA((2,)),
            pltpu.SemaphoreType.DMA((2,)),
            pltpu.SemaphoreType.DMA((peers - 1, pieces)),
            pltpu.SemaphoreType.DMA((peers - 1, pieces)),
        ],
        compiler_params=pltpu.CompilerParams(
            vmem_limit_bytes=40 << 20, collective_id=0, has_side_effects=True
        ),
        cost_estimate=pl.CostEstimate(
            flops=2 * planes * extent * right.shape[0] * right.shape[1],
            bytes_accessed=4 * planes * (2 * rows * lanes + extent * extent),
            transcendentals=0,
        ),
    )(columns, lines, weight, left, right)


def potential(density, extent, kernel_axes):
    size = lax.axis_size(kernel_axes)
    member = lax.axis_index(kernel_axes)
    band_count, slab_count = lax.axis_size("band"), lax.axis_size("slab")
    rows, columns = density.shape[:2]
    half = extent // 2 + 1
    each = -(-half // size)
    frequencies = np.arange(each * size)
    cosine, sine = np_phases(frequencies, np.arange(extent), extent)
    inside = (frequencies < half)[:, None]
    table = np.stack([cosine * inside, -sine * inside]).reshape(2, size, each, extent)
    forward = table.transpose(1, 0, 2, 3).reshape(-1, extent)
    weights = np.where((frequencies == 0) | (frequencies == extent // 2), 1.0, 2.0)
    backward = forward * np.tile(weights.reshape(size, 1, each), (1, 2, 1)).reshape(-1, 1)
    backward = backward / float(extent) ** 3
    forward = jnp.asarray(forward, jnp.float32)
    backward = jnp.asarray(backward, jnp.float32)
    lines = project("kz,pz->kp", forward, density.reshape(rows * columns, extent))
    planes = lax.all_to_all(lines, kernel_axes, split_axis=0, concat_axis=0, tiled=True)
    planes = planes.reshape(band_count, slab_count, 2 * each, rows, columns)
    planes = planes.transpose(2, 0, 3, 1, 4).reshape(2, each, extent, extent)
    cosine_table, sine_table = dft_tables(extent)
    real_part, imag_part = planes[0], planes[1]
    real_part, imag_part = rotate(real_part, imag_part, "kxy,yw->kxw", cosine_table, sine_table, -1.0)
    real_part, imag_part = rotate(real_part, imag_part, "kxy,xw->kwy", cosine_table, sine_table, -1.0)
    kernel = kernel_block(extent, (member * each, 0, 0), (each, extent, extent))
    real_part, imag_part = kernel * real_part, kernel * imag_part
    real_part, imag_part = rotate(real_part, imag_part, "kxy,xw->kwy", cosine_table, sine_table, 1.0)
    real_part, imag_part = rotate(real_part, imag_part, "kxy,yw->kxw", cosine_table, sine_table, 1.0)
    planes = jnp.stack((real_part, imag_part)).reshape(
        2 * each, band_count, rows, slab_count, columns
    )
    planes = planes.transpose(1, 3, 0, 2, 4).reshape(-1, rows * columns)
    lines = lax.all_to_all(planes, kernel_axes, split_axis=0, concat_axis=0, tiled=True)
    return project("kp,kz->pz", lines, backward).reshape(rows, columns, extent)


def quartered(wave_coeffs, column_mask, occupations, core_density):
    bands, _, rows, extent = wave_coeffs.shape[:4]
    quarter = extent // 4
    slab_index = lax.axis_index("slab")
    mask_rows = lax.dynamic_slice_in_dim(column_mask, slab_index * rows, rows, 0).astype(jnp.float32)
    kept = jnp.concatenate([mask_rows[:, :quarter], mask_rows[:, 3 * quarter :]], axis=1)
    lane_mask = jnp.tile(kept, (1, 2 * bands))
    columns = transform_columns(wave_coeffs, lane_mask, extent)
    cosine_table, sine_table = dft_tables(extent)
    inside = jnp.where(slab_index == 0, column_mask[0, quarter], 0).astype(jnp.float32)
    single = wave_coeffs[:, :, 0, quarter] * inside
    single_real, single_imag = rotate(
        single[:, 0], single[:, 1], "bz,zw->bw", cosine_table, sine_table, 1.0
    )
    phase_real, phase_imag = cosine_table[quarter], sine_table[quarter]
    line_real = single_real[..., None] * phase_real - single_imag[..., None] * phase_imag
    line_imag = single_real[..., None] * phase_imag + single_imag[..., None] * phase_real
    lines = jnp.concatenate([line_real, line_imag], axis=2).transpose(1, 0, 2)
    lines = lines.reshape(extent, bands * 2 * extent)
    bands_all = lax.axis_size("band") * bands
    weight = jnp.repeat(occupations / (float(extent) ** 3 * bands_all), 2 * extent)[None]
    summed = summed_density(columns, lines, weight, extent)
    turned = summed.transpose(2, 0, 1)
    turned = lax.all_to_all(turned, "slab", split_axis=0, concat_axis=1, tiled=True)
    density = turned.transpose(2, 0, 1)
    xc_potential = exchange_correlation(density + core_density)
    hartree = potential(density, extent, ("band", "slab"))
    return (hartree, xc_potential)


def solution(mesh):
    body = quartered if mesh.shape["slab"] == 4 else local
    return jax.shard_map(
        body,
        mesh=mesh,
        in_specs=(P("band", None, "slab", None, None), P(), P("band"), P("band", "slab", None)),
        out_specs=(P("band", "slab", None), P("band", "slab", None)),
        check_vma=False,
    )
```

```python
import math

import jax
import jax.numpy as jnp
import ml_dtypes
import numpy as np
from jax import lax
from jax.experimental import pallas as pl
from jax.experimental.pallas import tpu as pltpu
from jax.sharding import PartitionSpec as P

grid_spacing = 0.59
wigner_a = 0.44
wigner_b = 7.8


def dft_tables(extent):
    indices = jnp.arange(extent, dtype=jnp.int32)
    phase = indices[:, None] * indices[None, :] % extent
    angle = phase.astype(jnp.float32) * (2.0 * math.pi / extent)
    return (jnp.cos(angle), jnp.sin(angle))


def kernel_block(extent, starts, amounts):
    pieces = []
    for offset, amount in zip(starts, amounts):
        frequency = offset + jnp.arange(amount, dtype=jnp.int32)
        shifted = (frequency + extent // 2) % extent - extent // 2
        pieces.append(shifted * shifted)
    squared = pieces[0][:, None, None] + pieces[1][None, :, None] + pieces[2][None, None, :]
    length = extent * grid_spacing
    scaled = length * length / math.pi / jnp.maximum(squared, 1).astype(jnp.float32)
    return jnp.where(squared == 0, 0.0, scaled)


def exchange_correlation(density):
    root_density = jnp.cbrt(density)
    radius = (3.0 / (4.0 * math.pi)) ** (1.0 / 3.0) / root_density
    exchange_part = -((3.0 / math.pi) ** (1.0 / 3.0)) * root_density
    shifted = radius + wigner_b
    correlation = -wigner_a / shifted - wigner_a * radius / (3.0 * shifted * shifted)
    return exchange_part + correlation


def project(pattern, values, matrix):
    return jnp.einsum(pattern, values, matrix, precision=lax.Precision.HIGHEST)


def rotate(real_part, imag_part, pattern, cosine_table, sine_table, direction):
    new_real = project(pattern, real_part, cosine_table) - direction * project(
        pattern, imag_part, sine_table
    )
    new_imag = direction * project(pattern, real_part, sine_table) + project(
        pattern, imag_part, cosine_table
    )
    return (new_real, new_imag)


def local(wave_coeffs, column_mask, occupations, core_density):
    local_bands = wave_coeffs.shape[0]
    row_count = wave_coeffs.shape[2]
    extent = wave_coeffs.shape[3]
    bands_all = lax.axis_size("band") * local_bands
    band_rows = extent // lax.axis_size("band")
    slab_index = lax.axis_index("slab")
    band_index = lax.axis_index("band")
    cosine_table, sine_table = dft_tables(extent)
    mask_rows = lax.dynamic_slice_in_dim(column_mask, slab_index * row_count, row_count, 0).astype(
        jnp.float32
    )
    masked = wave_coeffs * mask_rows[None, None, :, :, None]
    real_part, imag_part = rotate(
        masked[:, 0], masked[:, 1], "bxyz,zw->bxyw", cosine_table, sine_table, 1.0
    )
    real_part, imag_part = rotate(
        real_part, imag_part, "bxyz,yw->bxwz", cosine_table, sine_table, 1.0
    )
    stacked = jnp.stack((real_part, imag_part), axis=1)
    factor = 1.0 / (float(extent) ** 3 * bands_all)
    partial_value = jnp.zeros((extent, row_count, extent), jnp.float32)
    for member in range(local_bands):
        arrived = lax.all_to_all(stacked[member], "slab", split_axis=2, concat_axis=1, tiled=True)
        plane_real, plane_imag = rotate(
            arrived[0], arrived[1], "xyz,xw->wyz", cosine_table, sine_table, 1.0
        )
        partial_value = partial_value + occupations[member] * (
            plane_real * plane_real + plane_imag * plane_imag
        )
    partial_value = partial_value * factor
    density = lax.psum(partial_value, "band")
    own_density = lax.dynamic_slice_in_dim(density, band_index * band_rows, band_rows, 0)
    first_real = project("xyz,zw->xyw", density, cosine_table)
    first_imag = -project("xyz,zw->xyw", density, sine_table)
    line_real, line_imag = rotate(
        first_real, first_imag, "xyz,xw->wyz", cosine_table, sine_table, -1.0
    )
    arrived = lax.all_to_all(
        jnp.stack((line_real, line_imag)), "slab", split_axis=1, concat_axis=2, tiled=True
    )
    line_real, line_imag = rotate(
        arrived[0], arrived[1], "xyz,yw->xwz", cosine_table, sine_table, -1.0
    )
    kernel = kernel_block(extent, (slab_index * row_count, 0, 0), (row_count, extent, extent))
    line_real, line_imag = rotate(
        kernel * line_real, kernel * line_imag, "xyz,yw->xwz", cosine_table, sine_table, 1.0
    )
    arrived = lax.all_to_all(
        jnp.stack((line_real, line_imag)), "slab", split_axis=2, concat_axis=1, tiled=True
    )
    cosine_rows = lax.dynamic_slice_in_dim(cosine_table, band_index * band_rows, band_rows, 1)
    sine_rows = lax.dynamic_slice_in_dim(sine_table, band_index * band_rows, band_rows, 1)
    line_real, line_imag = rotate(
        arrived[0], arrived[1], "xyz,xw->wyz", cosine_rows, sine_rows, 1.0
    )
    spatial = project("xyz,zw->xyw", line_real, cosine_table) - project(
        "xyz,zw->xyw", line_imag, sine_table
    )
    hartree = spatial / float(extent) ** 3
    xc_potential = exchange_correlation(own_density + core_density)
    return (hartree, xc_potential)


def split(values):
    high = values.astype(jnp.bfloat16)
    low = (values - high.astype(jnp.float32)).astype(jnp.bfloat16)
    return high, low


def full_dot(left, right):
    return jnp.dot(
        left, right, precision=lax.Precision.HIGHEST, preferred_element_type=jnp.float32
    )


def np_split(table):
    table = np.asarray(table, np.float32)
    high = table.astype(ml_dtypes.bfloat16)
    low = (table - high.astype(np.float32)).astype(ml_dtypes.bfloat16)
    return high, low


def np_phases(rows, columns, extent):
    angle = (np.outer(rows, columns) % extent) * (2.0 * np.pi / extent)
    return np.cos(angle), np.sin(angle)


def column_kernel(low_ref, high_ref, mask_ref, table_ref, out_ref):
    bands, _, rows = low_ref.shape[:3]
    for row in range(rows):
        parts = []
        for band in range(bands):
            pair = []
            for c in range(2):
                pair.append(
                    jnp.concatenate([low_ref[band, c, row], high_ref[band, c, row]], axis=0)
                )
            parts.append(pair)
        straight = jnp.concatenate([part for pair in parts for part in pair], axis=0)
        turned = jnp.concatenate([part for pair in parts for part in (-pair[1], pair[0])], axis=0)
        both = jnp.concatenate([straight, turned], axis=1)
        high, low = split(both)
        stacked = jnp.concatenate([high, low, high], axis=1)
        result = lax.dot_general(
            table_ref[...], stacked, (((1,), (1,)), ((), ())), preferred_element_type=jnp.float32
        )
        out_ref[:, row, :] = result * mask_ref[row : row + 1, :]


def transform_columns(wave_coeffs, lane_mask, extent):
    bands, _, rows = wave_coeffs.shape[:3]
    quarter = extent // 4
    lanes = bands * 2 * 2 * quarter
    indices = np.arange(extent)
    cosine, sine = np_phases(indices, indices, extent)
    high, low = np_split(np.concatenate([cosine, sine], axis=1))
    table = jnp.asarray(np.concatenate([high, high, low], axis=1))
    step = 8
    return pl.pallas_call(
        column_kernel,
        grid=(rows // step,),
        in_specs=[
            pl.BlockSpec((bands, 2, step, quarter, extent), lambda i: (0, 0, i, 0, 0)),
            pl.BlockSpec((bands, 2, step, quarter, extent), lambda i: (0, 0, i, 3, 0)),
            pl.BlockSpec((step, lanes), lambda i: (i, 0)),
            pl.BlockSpec((extent, 6 * extent), lambda i: (0, 0)),
        ],
        out_specs=pl.BlockSpec((extent, step, lanes), lambda i: (0, i, 0)),
        out_shape=jax.ShapeDtypeStruct((extent, rows, lanes), jnp.float32),
        compiler_params=pltpu.CompilerParams(vmem_limit_bytes=40 << 20),
        cost_estimate=pl.CostEstimate(
            flops=2 * rows * extent * lanes * 6 * extent,
            bytes_accessed=2 * 4 * extent * rows * lanes,
            transcendentals=0,
        ),
    )(wave_coeffs, wave_coeffs, lane_mask, table)


def density_kernel(
    columns_ref,
    lines_ref,
    weight_ref,
    left_ref,
    right_ref,
    depth_ref,
    across_ref,
    across_back_ref,
    along_ref,
    along_back_ref,
    density_ref,
    final_ref,
    land,
    extra,
    line,
    partial,
    shares,
    column_send,
    column_recv,
    small_send,
    small_recv,
    local_sem,
    share_send,
    share_recv,
    gathered,
    spectrum,
    rods,
    rods_out,
    returned,
    spread,
    columns_out,
    final,
    gather_send,
    gather_recv,
    band_send,
    band_recv,
    final_send,
    final_recv,
):
    mesh_ids = pl.DeviceIdType.MESH
    planes = line.shape[0]
    _, rows, extent = gathered.shape
    per_slab, each = spectrum.shape[1], rods.shape[1]
    peers = extent // rows
    pieces = column_recv.shape[1]
    step = planes // pieces
    band, slab = lax.axis_index("band"), lax.axis_index("slab")

    barrier = pltpu.get_barrier_semaphore()
    for shift in range(1, peers):
        pl.semaphore_signal(
            barrier, inc=1, device_id=((band + shift) % peers, slab), device_id_type=mesh_ids
        )
    for shift in range(1, 4):
        pl.semaphore_signal(
            barrier, inc=1, device_id=(band, (slab + shift) % 4), device_id_type=mesh_ids
        )
    pl.semaphore_wait(barrier, peers - 1 + 3)

    def column_copy(side, order, target, piece):
        return pltpu.make_async_remote_copy(
            src_ref=columns_ref.at[pl.ds(target * planes + piece * step, step)],
            dst_ref=land.at[side, pl.ds(piece * step, step)],
            send_sem=column_send.at[order, piece],
            recv_sem=column_recv.at[side, piece],
            device_id=(band, target),
            device_id_type=mesh_ids,
        )

    def line_copy(order, target):
        return pltpu.make_async_remote_copy(
            src_ref=lines_ref.at[pl.ds(target * planes, planes)],
            dst_ref=line,
            send_sem=small_send.at[order],
            recv_sem=small_recv.at[0],
            device_id=(band, target),
            device_id_type=mesh_ids,
        )

    def extra_copy(order, target):
        return pltpu.make_async_remote_copy(
            src_ref=columns_ref.at[pl.ds(target * planes, planes), pl.ds(0, 8)],
            dst_ref=extra,
            send_sem=small_send.at[order],
            recv_sem=small_recv.at[1],
            device_id=(band, target),
            device_id_type=mesh_ids,
        )

    def own_columns(side, slab_number):
        return pltpu.make_async_copy(
            columns_ref.at[pl.ds(slab_number * planes, planes)], land.at[side], local_sem.at[0]
        )

    def own_line():
        return pltpu.make_async_copy(lines_ref.at[pl.ds(0, planes)], line, local_sem.at[1])

    def own_extra():
        return pltpu.make_async_copy(
            columns_ref.at[pl.ds(planes, planes), pl.ds(0, 8)], extra, local_sem.at[1]
        )

    ends = ((0, 0, (3, 2, 1)), (1, 3, (0, 1, 2)))

    @pl.when(slab == 0)
    def _():
        for order, target in enumerate((3, 2, 1)):
            line_copy(order, target).start()
        own_line().start()

    @pl.when(slab == 1)
    def _():
        for order, target in enumerate((0, 2, 3)):
            extra_copy(order, target).start()
        own_extra().start()

    for side, number, targets in ends:

        @pl.when(slab == number)
        def _():
            for piece in range(pieces):
                for order, target in enumerate(targets):
                    column_copy(side, order, target, piece).start()
            own_columns(side, number).start()

    @pl.when(slab == 0)
    def _():
        own_line().wait()
        own_columns(0, 0).wait()

    @pl.when(slab != 0)
    def _():
        line_copy(0, 1).wait_recv()

    @pl.when(slab == 1)
    def _():
        own_extra().wait()

    @pl.when(slab != 1)
    def _():
        extra_copy(0, 2).wait_recv()

    @pl.when(slab == 3)
    def _():
        own_columns(1, 3).wait()

    def share_copy(shift, piece):
        peer = (band + shift) % peers
        return pltpu.make_async_remote_copy(
            src_ref=partial.at[
                pl.ds(piece * step, step), pl.ds(pl.multiple_of(peer * rows, rows), rows)
            ],
            dst_ref=shares.at[shift - 1, pl.ds(piece * step, step)],
            send_sem=share_send.at[shift - 1, piece],
            recv_sem=share_recv.at[shift - 1, piece],
            device_id=(peer, slab),
            device_id_type=mesh_ids,
        )

    def transform(plane, carry):
        filler = jnp.zeros((8, land.shape[3]), jnp.float32)
        values = jnp.concatenate([land[0, plane], land[1, plane], extra[plane], filler], axis=0)
        high, low = split(values)
        turned = jnp.dot(
            left_ref[...],
            jnp.concatenate([high, low, high], axis=0),
            preferred_element_type=jnp.float32,
        )
        wide = jnp.concatenate([turned[:extent], turned[extent:]], axis=1)
        high, low = split(wide)
        psi = jnp.dot(
            jnp.concatenate([high, low, high], axis=1),
            right_ref[...],
            preferred_element_type=jnp.float32,
        )
        psi = psi + line[pl.ds(plane, 1), :]
        square = psi * psi * weight_ref[...]
        total = square[:, :extent]
        for part in range(1, square.shape[1] // extent):
            total = total + square[:, part * extent : (part + 1) * extent]
        partial[plane] = total
        return carry

    def gather_copy(shift, piece):
        target = (slab + shift) % 4
        section = pl.ds(slab * planes + piece * step, step)
        return pltpu.make_async_remote_copy(
            src_ref=gathered.at[section],
            dst_ref=gathered.at[section],
            send_sem=gather_send.at[shift - 1, piece],
            recv_sem=gather_recv.at[shift - 1, piece],
            device_id=(band, target),
            device_id_type=mesh_ids,
        )

    def finish_piece(piece):
        section = pl.ds(piece * step, step)
        own = pl.ds(pl.multiple_of(band * rows, rows), rows)
        total = partial[section, own, :]
        for shift in range(1, peers):
            share_copy(shift, piece).wait_recv()
            total = total + shares[shift - 1, section]
        gathered[pl.ds(slab * planes + piece * step, step)] = total
        for shift in range(1, 4):
            gather_copy(shift, piece).start()

    for piece in range(pieces):

        @pl.when(slab != 0)
        def _():
            column_copy(0, 0, 1, piece).wait_recv()

        @pl.when(slab != 3)
        def _():
            column_copy(1, 0, 1, piece).wait_recv()

        lax.fori_loop(piece * step, (piece + 1) * step, transform, 0)
        for shift in range(1, peers):
            share_copy(shift, piece).start()
        if piece > 0:
            finish_piece(piece - 1)
    finish_piece(pieces - 1)

    for piece in range(pieces):
        for shift in range(1, 4):
            gather_copy(shift, piece).wait_recv()

    table = depth_ref[slab]
    for row in range(rows):
        lines = full_dot(table, gathered[:, row, :])
        returned[0, :, row, :] = lines[:per_slab]
        returned[1, :, row, :] = lines[per_slab:]

    def side_by_side(source):
        real_part = source[0].reshape(per_slab * rows, extent)
        imag_part = source[1].reshape(per_slab * rows, extent)
        return jnp.concatenate([real_part, imag_part], axis=1)

    result = full_dot(side_by_side(returned), along_ref[...])
    spectrum[0] = result[:, :extent].reshape(per_slab, rows, extent)
    spectrum[1] = result[:, extent:].reshape(per_slab, rows, extent)

    own_rows = pl.ds(pl.multiple_of(band * rows, rows), rows)

    def rods_copy(shift):
        peer = (band + shift) % peers
        return pltpu.make_async_remote_copy(
            src_ref=spectrum.at[:, pl.ds(peer * each, each)],
            dst_ref=rods.at[:, :, own_rows],
            send_sem=band_send.at[0, shift - 1],
            recv_sem=band_recv.at[0, shift - 1],
            device_id=(peer, slab),
            device_id_type=mesh_ids,
        )

    def return_copy(shift):
        peer = (band + shift) % peers
        return pltpu.make_async_remote_copy(
            src_ref=rods_out.at[:, :, pl.ds(pl.multiple_of(peer * rows, rows), rows)],
            dst_ref=spread.at[:, pl.ds(band * each, each)],
            send_sem=band_send.at[1, shift - 1],
            recv_sem=band_recv.at[1, shift - 1],
            device_id=(peer, slab),
            device_id_type=mesh_ids,
        )

    for shift in range(1, peers):
        rods_copy(shift).start()
    rods[:, :, own_rows, :] = spectrum[:, pl.ds(band * each, each)]
    density_ref[...] = gathered[...]
    for shift in range(1, peers):
        rods_copy(shift).wait_recv()

    def squares(dimension):
        index = lax.broadcasted_iota(jnp.int32, (extent, extent), dimension)
        shifted = jnp.where(index >= extent // 2, index - extent, index)
        return shifted * shifted

    flat = squares(0) + squares(1)
    length = extent * grid_spacing
    for item in range(each):
        stacked = jnp.concatenate([rods[0, item], rods[1, item]], axis=0)
        lines = full_dot(across_ref[...], stacked)
        frequency = slab * per_slab + band * each + item
        squared = flat + frequency * frequency
        kernel = (length * length / math.pi) / jnp.maximum(squared, 1).astype(jnp.float32)
        kernel = jnp.where(squared == 0, 0.0, kernel)
        high, low = split(lines * jnp.concatenate([kernel, kernel], axis=0))
        lines = jnp.dot(
            across_back_ref[...],
            jnp.concatenate([high, low, high], axis=0),
            preferred_element_type=jnp.float32,
        )
        rods_out[0, item] = lines[:extent]
        rods_out[1, item] = lines[extent:]

    for shift in range(1, peers):
        return_copy(shift).start()
    spread[:, pl.ds(band * each, each)] = rods_out[:, :, own_rows, :]
    for shift in range(1, peers):
        return_copy(shift).wait_recv()

    high, low = split(side_by_side(spread))
    result = jnp.dot(
        jnp.concatenate([high, low, high], axis=1),
        along_back_ref[...],
        preferred_element_type=jnp.float32,
    )
    half = per_slab * rows
    for c in range(2):
        flipped = result[:, c * extent : (c + 1) * extent].T
        columns_out[:, c * half : (c + 1) * half] = flipped

    def final_copy(shift):
        target = (slab + shift) % 4
        return pltpu.make_async_remote_copy(
            src_ref=columns_out.at[pl.ds(pl.multiple_of(target * planes, planes), planes)],
            dst_ref=final.at[slab],
            send_sem=final_send.at[shift - 1],
            recv_sem=final_recv.at[shift - 1],
            device_id=(band, target),
            device_id_type=mesh_ids,
        )

    for shift in range(1, 4):
        final_copy(shift).start()
    final[slab] = columns_out[pl.ds(pl.multiple_of(slab * planes, planes), planes)]
    for shift in range(1, 4):
        final_copy(shift).wait_recv()
    final_ref[...] = final[...]

    for shift in range(1, peers):
        rods_copy(shift).wait_send()
        return_copy(shift).wait_send()
    for shift in range(1, 4):
        final_copy(shift).wait_send()
        for piece in range(pieces):
            gather_copy(shift, piece).wait_send()
    for piece in range(pieces):
        for shift in range(1, peers):
            share_copy(shift, piece).wait_send()
    for side, number, targets in ends:

        @pl.when(slab == number)
        def _():
            for piece in range(pieces):
                for order, target in enumerate(targets):
                    column_copy(side, order, target, piece).wait_send()

    @pl.when(slab == 0)
    def _():
        for order, target in enumerate((3, 2, 1)):
            line_copy(order, target).wait_send()

    @pl.when(slab == 1)
    def _():
        for order, target in enumerate((0, 2, 3)):
            extra_copy(order, target).wait_send()


def plane_tables(bands, extent):
    quarter = extent // 4
    indices = np.arange(extent)
    kept = np.concatenate([np.arange(quarter), np.arange(3 * quarter, extent)])
    count = 2 * quarter
    cosine, sine = np_phases(indices, np.concatenate([kept, [quarter]]), extent)
    left = np.zeros((2 * extent, count + 16))
    left[:extent, : count + 1] = cosine
    left[extent:, : count + 1] = sine
    high, low = np_split(left)
    left = np.concatenate([high, high, low], axis=1)
    cosine, sine = np_phases(kept, indices, extent)
    lanes = bands * 2 * count
    right = np.zeros((2, bands, 2, count, bands, 2, extent))
    for band in range(bands):
        right[0, band, 0, :, band, 0] = cosine
        right[0, band, 1, :, band, 0] = -sine
        right[1, band, 0, :, band, 0] = -sine
        right[1, band, 1, :, band, 0] = -cosine
        right[0, band, 0, :, band, 1] = sine
        right[0, band, 1, :, band, 1] = cosine
        right[1, band, 0, :, band, 1] = cosine
        right[1, band, 1, :, band, 1] = -sine
    high, low = np_split(right.reshape(2 * lanes, bands * 2 * extent))
    right = np.concatenate([high, high, low], axis=0)
    return jnp.asarray(left), jnp.asarray(right)


def line_tables(extent, slabs, peers):
    half = extent // 2 + 1
    per_slab = -(-half // (slabs * peers)) * peers
    indices = np.arange(extent)
    frequencies = np.arange(slabs * per_slab)
    cosine, sine = np_phases(frequencies, indices, extent)
    inside = (frequencies < half)[:, None]
    table = np.stack([cosine * inside, -sine * inside]).reshape(2, slabs, per_slab, extent)
    table = table.transpose(1, 0, 2, 3)
    counts = np.where((frequencies == 0) | (frequencies == extent // 2), 1.0, 2.0)
    backward = table * counts.reshape(slabs, 1, per_slab, 1) / float(extent) ** 3
    depth = table.reshape(slabs, 2 * per_slab, extent)
    cosine, sine = np_phases(indices, indices, extent)
    across = np.block([[cosine, sine], [-sine, cosine]])
    high, low = np_split(across.T)
    across_back = np.concatenate([high, high, low], axis=1)
    high, low = np_split(across)
    along_back = np.concatenate([high, high, low], axis=0)
    return (
        jnp.asarray(depth, jnp.float32),
        jnp.asarray(across, jnp.float32),
        jnp.asarray(across_back),
        jnp.asarray(across.T, jnp.float32),
        jnp.asarray(along_back),
        jnp.asarray(backward, jnp.float32),
    )


def summed_density(columns, lines, weight, extent):
    _, rows, lanes = columns.shape
    bands = lines.shape[1] // (2 * extent)
    planes = extent // 4
    peers = lax.axis_size("band")
    share = extent // peers
    left, right = plane_tables(bands, extent)
    *tables, backward = line_tables(extent, 4, peers)
    per_slab = tables[0].shape[1] // 2
    each = per_slab // peers
    pieces = 4
    vmem = pl.BlockSpec(memory_space=pltpu.VMEM)
    density, final = pl.pallas_call(
        density_kernel,
        in_specs=[pl.BlockSpec(memory_space=pl.ANY)] + [vmem] * 9,
        out_specs=(vmem, vmem),
        out_shape=(
            jax.ShapeDtypeStruct((extent, share, extent), jnp.float32),
            jax.ShapeDtypeStruct((4, planes, 2 * per_slab * share), jnp.float32),
        ),
        scratch_shapes=[
            pltpu.VMEM((2, planes, rows, lanes), jnp.float32),
            pltpu.VMEM((planes, 8, lanes), jnp.float32),
            pltpu.VMEM((planes, lines.shape[1]), jnp.float32),
            pltpu.VMEM((planes, extent, extent), jnp.float32),
            pltpu.VMEM((peers - 1, planes, share, extent), jnp.float32),
            pltpu.SemaphoreType.DMA((3, pieces)),
            pltpu.SemaphoreType.DMA((2, pieces)),
            pltpu.SemaphoreType.DMA((3,)),
            pltpu.SemaphoreType.DMA((2,)),
            pltpu.SemaphoreType.DMA((2,)),
            pltpu.SemaphoreType.DMA((peers - 1, pieces)),
            pltpu.SemaphoreType.DMA((peers - 1, pieces)),
            pltpu.VMEM((extent, share, extent), jnp.float32),
            pltpu.VMEM((2, per_slab, share, extent), jnp.float32),
            pltpu.VMEM((2, each, extent, extent), jnp.float32),
            pltpu.VMEM((2, each, extent, extent), jnp.float32),
            pltpu.VMEM((2, per_slab, share, extent), jnp.float32),
            pltpu.VMEM((2, per_slab, share, extent), jnp.float32),
            pltpu.VMEM((extent, 2 * per_slab * share), jnp.float32),
            pltpu.VMEM((4, planes, 2 * per_slab * share), jnp.float32),
            pltpu.SemaphoreType.DMA((3, pieces)),
            pltpu.SemaphoreType.DMA((3, pieces)),
            pltpu.SemaphoreType.DMA((2, peers - 1)),
            pltpu.SemaphoreType.DMA((2, peers - 1)),
            pltpu.SemaphoreType.DMA((3,)),
            pltpu.SemaphoreType.DMA((3,)),
        ],
        compiler_params=pltpu.CompilerParams(
            vmem_limit_bytes=40 << 20, collective_id=0, has_side_effects=True
        ),
        cost_estimate=pl.CostEstimate(
            flops=2 * planes * extent * right.shape[0] * right.shape[1],
            bytes_accessed=4 * planes * (2 * rows * lanes + extent * extent),
            transcendentals=0,
        ),
    )(columns, lines, weight, left, right, *tables)
    final = final.reshape(4, planes, 2, per_slab, share)
    hartree = jnp.einsum("syckx,sckz->xyz", final, backward, precision=lax.Precision.HIGHEST)
    own = lax.dynamic_slice_in_dim(density, lax.axis_index("slab") * planes, planes, 2)
    return hartree, own.transpose(1, 2, 0)


def quartered(wave_coeffs, column_mask, occupations, core_density):
    bands, _, rows, extent = wave_coeffs.shape[:4]
    quarter = extent // 4
    slab_index = lax.axis_index("slab")
    mask_rows = lax.dynamic_slice_in_dim(column_mask, slab_index * rows, rows, 0).astype(jnp.float32)
    kept = jnp.concatenate([mask_rows[:, :quarter], mask_rows[:, 3 * quarter :]], axis=1)
    lane_mask = jnp.tile(kept, (1, 2 * bands))
    columns = transform_columns(wave_coeffs, lane_mask, extent)
    cosine_table, sine_table = dft_tables(extent)
    inside = jnp.where(slab_index == 0, column_mask[0, quarter], 0).astype(jnp.float32)
    single = wave_coeffs[:, :, 0, quarter] * inside
    single_real, single_imag = rotate(
        single[:, 0], single[:, 1], "bz,zw->bw", cosine_table, sine_table, 1.0
    )
    phase_real, phase_imag = cosine_table[quarter], sine_table[quarter]
    line_real = single_real[..., None] * phase_real - single_imag[..., None] * phase_imag
    line_imag = single_real[..., None] * phase_imag + single_imag[..., None] * phase_real
    lines = jnp.concatenate([line_real, line_imag], axis=2).transpose(1, 0, 2)
    lines = lines.reshape(extent, bands * 2 * extent)
    bands_all = lax.axis_size("band") * bands
    weight = jnp.repeat(occupations / (float(extent) ** 3 * bands_all), 2 * extent)[None]
    hartree, density = summed_density(columns, lines, weight, extent)
    xc_potential = exchange_correlation(density + core_density)
    return (hartree, xc_potential)


def solution(mesh):
    body = quartered if mesh.shape["slab"] == 4 else local
    return jax.shard_map(
        body,
        mesh=mesh,
        in_specs=(P("band", None, "slab", None, None), P(), P("band"), P("band", "slab", None)),
        out_specs=(P("band", "slab", None), P("band", "slab", None)),
        check_vma=False,
    )
```

```python
import math

import jax
import jax.numpy as jnp
import ml_dtypes
import numpy as np
from jax import lax
from jax.experimental import pallas as pl
from jax.experimental.pallas import tpu as pltpu
from jax.sharding import PartitionSpec as P

grid_spacing = 0.59
wigner_a = 0.44
wigner_b = 7.8


def dft_tables(extent):
    indices = jnp.arange(extent, dtype=jnp.int32)
    phase = indices[:, None] * indices[None, :] % extent
    angle = phase.astype(jnp.float32) * (2.0 * math.pi / extent)
    return (jnp.cos(angle), jnp.sin(angle))


def kernel_block(extent, starts, amounts):
    pieces = []
    for offset, amount in zip(starts, amounts):
        frequency = offset + jnp.arange(amount, dtype=jnp.int32)
        shifted = (frequency + extent // 2) % extent - extent // 2
        pieces.append(shifted * shifted)
    squared = pieces[0][:, None, None] + pieces[1][None, :, None] + pieces[2][None, None, :]
    length = extent * grid_spacing
    scaled = length * length / math.pi / jnp.maximum(squared, 1).astype(jnp.float32)
    return jnp.where(squared == 0, 0.0, scaled)


def exchange_correlation(density):
    root_density = jnp.cbrt(density)
    radius = (3.0 / (4.0 * math.pi)) ** (1.0 / 3.0) / root_density
    exchange_part = -((3.0 / math.pi) ** (1.0 / 3.0)) * root_density
    shifted = radius + wigner_b
    correlation = -wigner_a / shifted - wigner_a * radius / (3.0 * shifted * shifted)
    return exchange_part + correlation


def project(pattern, values, matrix):
    return jnp.einsum(pattern, values, matrix, precision=lax.Precision.HIGHEST)


def rotate(real_part, imag_part, pattern, cosine_table, sine_table, direction):
    new_real = project(pattern, real_part, cosine_table) - direction * project(
        pattern, imag_part, sine_table
    )
    new_imag = direction * project(pattern, real_part, sine_table) + project(
        pattern, imag_part, cosine_table
    )
    return (new_real, new_imag)


def local(wave_coeffs, column_mask, occupations, core_density):
    local_bands = wave_coeffs.shape[0]
    row_count = wave_coeffs.shape[2]
    extent = wave_coeffs.shape[3]
    bands_all = lax.axis_size("band") * local_bands
    band_rows = extent // lax.axis_size("band")
    slab_index = lax.axis_index("slab")
    band_index = lax.axis_index("band")
    cosine_table, sine_table = dft_tables(extent)
    mask_rows = lax.dynamic_slice_in_dim(column_mask, slab_index * row_count, row_count, 0).astype(
        jnp.float32
    )
    masked = wave_coeffs * mask_rows[None, None, :, :, None]
    real_part, imag_part = rotate(
        masked[:, 0], masked[:, 1], "bxyz,zw->bxyw", cosine_table, sine_table, 1.0
    )
    real_part, imag_part = rotate(
        real_part, imag_part, "bxyz,yw->bxwz", cosine_table, sine_table, 1.0
    )
    stacked = jnp.stack((real_part, imag_part), axis=1)
    factor = 1.0 / (float(extent) ** 3 * bands_all)
    partial_value = jnp.zeros((extent, row_count, extent), jnp.float32)
    for member in range(local_bands):
        arrived = lax.all_to_all(stacked[member], "slab", split_axis=2, concat_axis=1, tiled=True)
        plane_real, plane_imag = rotate(
            arrived[0], arrived[1], "xyz,xw->wyz", cosine_table, sine_table, 1.0
        )
        partial_value = partial_value + occupations[member] * (
            plane_real * plane_real + plane_imag * plane_imag
        )
    partial_value = partial_value * factor
    density = lax.psum(partial_value, "band")
    own_density = lax.dynamic_slice_in_dim(density, band_index * band_rows, band_rows, 0)
    first_real = project("xyz,zw->xyw", density, cosine_table)
    first_imag = -project("xyz,zw->xyw", density, sine_table)
    line_real, line_imag = rotate(
        first_real, first_imag, "xyz,xw->wyz", cosine_table, sine_table, -1.0
    )
    arrived = lax.all_to_all(
        jnp.stack((line_real, line_imag)), "slab", split_axis=1, concat_axis=2, tiled=True
    )
    line_real, line_imag = rotate(
        arrived[0], arrived[1], "xyz,yw->xwz", cosine_table, sine_table, -1.0
    )
    kernel = kernel_block(extent, (slab_index * row_count, 0, 0), (row_count, extent, extent))
    line_real, line_imag = rotate(
        kernel * line_real, kernel * line_imag, "xyz,yw->xwz", cosine_table, sine_table, 1.0
    )
    arrived = lax.all_to_all(
        jnp.stack((line_real, line_imag)), "slab", split_axis=2, concat_axis=1, tiled=True
    )
    cosine_rows = lax.dynamic_slice_in_dim(cosine_table, band_index * band_rows, band_rows, 1)
    sine_rows = lax.dynamic_slice_in_dim(sine_table, band_index * band_rows, band_rows, 1)
    line_real, line_imag = rotate(
        arrived[0], arrived[1], "xyz,xw->wyz", cosine_rows, sine_rows, 1.0
    )
    spatial = project("xyz,zw->xyw", line_real, cosine_table) - project(
        "xyz,zw->xyw", line_imag, sine_table
    )
    hartree = spatial / float(extent) ** 3
    xc_potential = exchange_correlation(own_density + core_density)
    return (hartree, xc_potential)


def split(values):
    high = values.astype(jnp.bfloat16)
    low = (values - high.astype(jnp.float32)).astype(jnp.bfloat16)
    return high, low


def full_dot(left, right):
    return jnp.dot(
        left, right, precision=lax.Precision.HIGHEST, preferred_element_type=jnp.float32
    )


def np_split(table):
    table = np.asarray(table, np.float32)
    high = table.astype(ml_dtypes.bfloat16)
    low = (table - high.astype(np.float32)).astype(ml_dtypes.bfloat16)
    return high, low


def np_phases(rows, columns, extent):
    angle = (np.outer(rows, columns) % extent) * (2.0 * np.pi / extent)
    return np.cos(angle), np.sin(angle)


def column_kernel(low_ref, high_ref, mask_ref, table_ref, out_ref):
    bands, _, rows = low_ref.shape[:3]
    for row in range(rows):
        parts = []
        for band in range(bands):
            pair = []
            for c in range(2):
                pair.append(
                    jnp.concatenate([low_ref[band, c, row], high_ref[band, c, row]], axis=0)
                )
            parts.append(pair)
        straight = jnp.concatenate([part for pair in parts for part in pair], axis=0)
        turned = jnp.concatenate([part for pair in parts for part in (-pair[1], pair[0])], axis=0)
        both = jnp.concatenate([straight, turned], axis=1)
        high, low = split(both)
        stacked = jnp.concatenate([high, low, high], axis=1)
        result = lax.dot_general(
            table_ref[...], stacked, (((1,), (1,)), ((), ())), preferred_element_type=jnp.float32
        )
        out_ref[:, row, :] = result * mask_ref[row : row + 1, :]


def transform_columns(wave_coeffs, lane_mask, extent):
    bands, _, rows = wave_coeffs.shape[:3]
    quarter = extent // 4
    lanes = bands * 2 * 2 * quarter
    indices = np.arange(extent)
    cosine, sine = np_phases(indices, indices, extent)
    high, low = np_split(np.concatenate([cosine, sine], axis=1))
    table = jnp.asarray(np.concatenate([high, high, low], axis=1))
    step = 8
    return pl.pallas_call(
        column_kernel,
        grid=(rows // step,),
        in_specs=[
            pl.BlockSpec((bands, 2, step, quarter, extent), lambda i: (0, 0, i, 0, 0)),
            pl.BlockSpec((bands, 2, step, quarter, extent), lambda i: (0, 0, i, 3, 0)),
            pl.BlockSpec((step, lanes), lambda i: (i, 0)),
            pl.BlockSpec((extent, 6 * extent), lambda i: (0, 0)),
        ],
        out_specs=pl.BlockSpec((extent, step, lanes), lambda i: (0, i, 0)),
        out_shape=jax.ShapeDtypeStruct((extent, rows, lanes), jnp.float32),
        compiler_params=pltpu.CompilerParams(vmem_limit_bytes=40 << 20),
        cost_estimate=pl.CostEstimate(
            flops=2 * rows * extent * lanes * 6 * extent,
            bytes_accessed=2 * 4 * extent * rows * lanes,
            transcendentals=0,
        ),
    )(wave_coeffs, wave_coeffs, lane_mask, table)


def density_kernel(
    columns_ref,
    lines_ref,
    weight_ref,
    left_ref,
    right_ref,
    depth_ref,
    across_ref,
    across_back_ref,
    along_ref,
    along_back_ref,
    density_ref,
    final_ref,
    land,
    extra,
    line,
    partial,
    shares,
    column_send,
    column_recv,
    small_send,
    small_recv,
    local_sem,
    share_send,
    share_recv,
    gathered,
    spectrum,
    rods,
    rods_out,
    returned,
    spread,
    columns_out,
    final,
    gather_send,
    gather_recv,
    band_send,
    band_recv,
    final_send,
    final_recv,
):
    mesh_ids = pl.DeviceIdType.MESH
    planes = line.shape[0]
    _, rows, extent = gathered.shape
    per_slab, each = spectrum.shape[1], rods.shape[1]
    peers = extent // rows
    pieces = column_recv.shape[1]
    step = planes // pieces
    band, slab = lax.axis_index("band"), lax.axis_index("slab")

    barrier = pltpu.get_barrier_semaphore()
    for shift in range(1, peers):
        pl.semaphore_signal(
            barrier, inc=1, device_id=((band + shift) % peers, slab), device_id_type=mesh_ids
        )
    for shift in range(1, 4):
        pl.semaphore_signal(
            barrier, inc=1, device_id=(band, (slab + shift) % 4), device_id_type=mesh_ids
        )
    pl.semaphore_wait(barrier, peers - 1 + 3)

    def column_copy(side, order, target, piece):
        return pltpu.make_async_remote_copy(
            src_ref=columns_ref.at[pl.ds(target * planes + piece * step, step)],
            dst_ref=land.at[side, pl.ds(piece * step, step)],
            send_sem=column_send.at[order, piece],
            recv_sem=column_recv.at[side, piece],
            device_id=(band, target),
            device_id_type=mesh_ids,
        )

    def line_copy(order, target):
        return pltpu.make_async_remote_copy(
            src_ref=lines_ref.at[pl.ds(target * planes, planes)],
            dst_ref=line,
            send_sem=small_send.at[order],
            recv_sem=small_recv.at[0],
            device_id=(band, target),
            device_id_type=mesh_ids,
        )

    def extra_copy(order, target):
        return pltpu.make_async_remote_copy(
            src_ref=columns_ref.at[pl.ds(target * planes, planes), pl.ds(0, 8)],
            dst_ref=extra,
            send_sem=small_send.at[order],
            recv_sem=small_recv.at[1],
            device_id=(band, target),
            device_id_type=mesh_ids,
        )

    def own_columns(side, slab_number):
        return pltpu.make_async_copy(
            columns_ref.at[pl.ds(slab_number * planes, planes)], land.at[side], local_sem.at[0]
        )

    def own_line():
        return pltpu.make_async_copy(lines_ref.at[pl.ds(0, planes)], line, local_sem.at[1])

    def own_extra():
        return pltpu.make_async_copy(
            columns_ref.at[pl.ds(planes, planes), pl.ds(0, 8)], extra, local_sem.at[1]
        )

    ends = ((0, 0, (3, 2, 1)), (1, 3, (0, 1, 2)))

    @pl.when(slab == 0)
    def _():
        for order, target in enumerate((3, 2, 1)):
            line_copy(order, target).start()
        own_line().start()

    @pl.when(slab == 1)
    def _():
        for order, target in enumerate((0, 2, 3)):
            extra_copy(order, target).start()
        own_extra().start()

    for side, number, targets in ends:

        @pl.when(slab == number)
        def _():
            for piece in range(pieces):
                for order, target in enumerate(targets):
                    column_copy(side, order, target, piece).start()
            own_columns(side, number).start()

    @pl.when(slab == 0)
    def _():
        own_line().wait()
        own_columns(0, 0).wait()

    @pl.when(slab != 0)
    def _():
        line_copy(0, 1).wait_recv()

    @pl.when(slab == 1)
    def _():
        own_extra().wait()

    @pl.when(slab != 1)
    def _():
        extra_copy(0, 2).wait_recv()

    @pl.when(slab == 3)
    def _():
        own_columns(1, 3).wait()

    def share_copy(shift, piece):
        peer = (band + shift) % peers
        return pltpu.make_async_remote_copy(
            src_ref=partial.at[
                pl.ds(piece * step, step), pl.ds(pl.multiple_of(peer * rows, rows), rows)
            ],
            dst_ref=shares.at[shift - 1, pl.ds(piece * step, step)],
            send_sem=share_send.at[shift - 1, piece],
            recv_sem=share_recv.at[shift - 1, piece],
            device_id=(peer, slab),
            device_id_type=mesh_ids,
        )

    def transform(plane, carry):
        filler = jnp.zeros((8, land.shape[3]), jnp.float32)
        values = jnp.concatenate([land[0, plane], land[1, plane], extra[plane], filler], axis=0)
        high, low = split(values)
        turned = jnp.dot(
            left_ref[...],
            jnp.concatenate([high, low, high], axis=0),
            preferred_element_type=jnp.float32,
        )
        wide = jnp.concatenate([turned[:extent], turned[extent:]], axis=1)
        high, low = split(wide)
        psi = jnp.dot(
            jnp.concatenate([high, low, high], axis=1),
            right_ref[...],
            preferred_element_type=jnp.float32,
        )
        psi = psi + line[pl.ds(plane, 1), :]
        square = psi * psi * weight_ref[...]
        total = square[:, :extent]
        for part in range(1, square.shape[1] // extent):
            total = total + square[:, part * extent : (part + 1) * extent]
        partial[plane] = total
        return carry

    def gather_copy(shift, piece):
        target = (slab + shift) % 4
        section = pl.ds(slab * planes + piece * step, step)
        return pltpu.make_async_remote_copy(
            src_ref=gathered.at[section],
            dst_ref=gathered.at[section],
            send_sem=gather_send.at[shift - 1, piece],
            recv_sem=gather_recv.at[shift - 1, piece],
            device_id=(band, target),
            device_id_type=mesh_ids,
        )

    def finish_piece(piece):
        section = pl.ds(piece * step, step)
        own = pl.ds(pl.multiple_of(band * rows, rows), rows)
        total = partial[section, own, :]
        for shift in range(1, peers):
            share_copy(shift, piece).wait_recv()
            total = total + shares[shift - 1, section]
        gathered[pl.ds(slab * planes + piece * step, step)] = total
        for shift in range(1, 4):
            gather_copy(shift, piece).start()

    for piece in range(pieces):

        @pl.when(slab != 0)
        def _():
            column_copy(0, 0, 1, piece).wait_recv()

        @pl.when(slab != 3)
        def _():
            column_copy(1, 0, 1, piece).wait_recv()

        lax.fori_loop(piece * step, (piece + 1) * step, transform, 0)
        for shift in range(1, peers):
            share_copy(shift, piece).start()
        if piece > 0:
            finish_piece(piece - 1)
    finish_piece(pieces - 1)

    for piece in range(pieces):
        for shift in range(1, 4):
            gather_copy(shift, piece).wait_recv()

    table = depth_ref[slab]
    for row in range(rows):
        lines = full_dot(table, gathered[:, row, :])
        returned[0, :, row, :] = lines[:per_slab]
        returned[1, :, row, :] = lines[per_slab:]

    def side_by_side(source):
        real_part = source[0].reshape(per_slab * rows, extent)
        imag_part = source[1].reshape(per_slab * rows, extent)
        return jnp.concatenate([real_part, imag_part], axis=1)

    result = full_dot(side_by_side(returned), along_ref[...])
    spectrum[0] = result[:, :extent].reshape(per_slab, rows, extent)
    spectrum[1] = result[:, extent:].reshape(per_slab, rows, extent)

    own_rows = pl.ds(pl.multiple_of(band * rows, rows), rows)

    def rods_copy(shift):
        peer = (band + shift) % peers
        return pltpu.make_async_remote_copy(
            src_ref=spectrum.at[:, pl.ds(peer * each, each)],
            dst_ref=rods.at[:, :, own_rows],
            send_sem=band_send.at[0, shift - 1],
            recv_sem=band_recv.at[0, shift - 1],
            device_id=(peer, slab),
            device_id_type=mesh_ids,
        )

    def return_copy(shift):
        peer = (band + shift) % peers
        return pltpu.make_async_remote_copy(
            src_ref=rods_out.at[:, :, pl.ds(pl.multiple_of(peer * rows, rows), rows)],
            dst_ref=spread.at[:, pl.ds(band * each, each)],
            send_sem=band_send.at[1, shift - 1],
            recv_sem=band_recv.at[1, shift - 1],
            device_id=(peer, slab),
            device_id_type=mesh_ids,
        )

    for shift in range(1, peers):
        rods_copy(shift).start()
    rods[:, :, own_rows, :] = spectrum[:, pl.ds(band * each, each)]
    density_ref[...] = gathered[...]
    for shift in range(1, peers):
        rods_copy(shift).wait_recv()

    def squares(dimension):
        index = lax.broadcasted_iota(jnp.int32, (extent, extent), dimension)
        shifted = jnp.where(index >= extent // 2, index - extent, index)
        return shifted * shifted

    flat = squares(0) + squares(1)
    length = extent * grid_spacing
    for item in range(each):
        stacked = jnp.concatenate([rods[0, item], rods[1, item]], axis=0)
        lines = full_dot(across_ref[...], stacked)
        frequency = slab * per_slab + band * each + item
        squared = flat + frequency * frequency
        kernel = (length * length / math.pi) / jnp.maximum(squared, 1).astype(jnp.float32)
        kernel = jnp.where(squared == 0, 0.0, kernel)
        high, low = split(lines * jnp.concatenate([kernel, kernel], axis=0))
        lines = jnp.dot(
            across_back_ref[...],
            jnp.concatenate([high, low, high], axis=0),
            preferred_element_type=jnp.float32,
        )
        rods_out[0, item] = lines[:extent]
        rods_out[1, item] = lines[extent:]

    for shift in range(1, peers):
        return_copy(shift).start()
    spread[:, pl.ds(band * each, each)] = rods_out[:, :, own_rows, :]
    for shift in range(1, peers):
        return_copy(shift).wait_recv()

    high, low = split(side_by_side(spread))
    result = jnp.dot(
        jnp.concatenate([high, low, high], axis=1),
        along_back_ref[...],
        preferred_element_type=jnp.float32,
    )
    half = per_slab * rows
    for c in range(2):
        flipped = result[:, c * extent : (c + 1) * extent].T
        columns_out[:, c * half : (c + 1) * half] = flipped

    def final_copy(shift):
        target = (slab + shift) % 4
        return pltpu.make_async_remote_copy(
            src_ref=columns_out.at[pl.ds(pl.multiple_of(target * planes, planes), planes)],
            dst_ref=final.at[slab],
            send_sem=final_send.at[shift - 1],
            recv_sem=final_recv.at[shift - 1],
            device_id=(band, target),
            device_id_type=mesh_ids,
        )

    for shift in range(1, 4):
        final_copy(shift).start()
    final[slab] = columns_out[pl.ds(pl.multiple_of(slab * planes, planes), planes)]
    for shift in range(1, 4):
        final_copy(shift).wait_recv()
    final_ref[...] = final[...]

    for shift in range(1, peers):
        rods_copy(shift).wait_send()
        return_copy(shift).wait_send()
    for shift in range(1, 4):
        final_copy(shift).wait_send()
        for piece in range(pieces):
            gather_copy(shift, piece).wait_send()
    for piece in range(pieces):
        for shift in range(1, peers):
            share_copy(shift, piece).wait_send()
    for side, number, targets in ends:

        @pl.when(slab == number)
        def _():
            for piece in range(pieces):
                for order, target in enumerate(targets):
                    column_copy(side, order, target, piece).wait_send()

    @pl.when(slab == 0)
    def _():
        for order, target in enumerate((3, 2, 1)):
            line_copy(order, target).wait_send()

    @pl.when(slab == 1)
    def _():
        for order, target in enumerate((0, 2, 3)):
            extra_copy(order, target).wait_send()


def plane_tables(bands, extent):
    quarter = extent // 4
    indices = np.arange(extent)
    kept = np.concatenate([np.arange(quarter), np.arange(3 * quarter, extent)])
    count = 2 * quarter
    cosine, sine = np_phases(indices, np.concatenate([kept, [quarter]]), extent)
    left = np.zeros((2 * extent, count + 16))
    left[:extent, : count + 1] = cosine
    left[extent:, : count + 1] = sine
    high, low = np_split(left)
    left = np.concatenate([high, high, low], axis=1)
    cosine, sine = np_phases(kept, indices, extent)
    lanes = bands * 2 * count
    right = np.zeros((2, bands, 2, count, bands, 2, extent))
    for band in range(bands):
        right[0, band, 0, :, band, 0] = cosine
        right[0, band, 1, :, band, 0] = -sine
        right[1, band, 0, :, band, 0] = -sine
        right[1, band, 1, :, band, 0] = -cosine
        right[0, band, 0, :, band, 1] = sine
        right[0, band, 1, :, band, 1] = cosine
        right[1, band, 0, :, band, 1] = cosine
        right[1, band, 1, :, band, 1] = -sine
    high, low = np_split(right.reshape(2 * lanes, bands * 2 * extent))
    right = np.concatenate([high, high, low], axis=0)
    return jnp.asarray(left), jnp.asarray(right)


def line_tables(extent, slabs, peers):
    half = extent // 2 + 1
    per_slab = -(-half // (slabs * peers)) * peers
    indices = np.arange(extent)
    frequencies = np.arange(slabs * per_slab)
    cosine, sine = np_phases(frequencies, indices, extent)
    inside = (frequencies < half)[:, None]
    table = np.stack([cosine * inside, -sine * inside]).reshape(2, slabs, per_slab, extent)
    table = table.transpose(1, 0, 2, 3)
    counts = np.where((frequencies == 0) | (frequencies == extent // 2), 1.0, 2.0)
    backward = table * counts.reshape(slabs, 1, per_slab, 1) / float(extent) ** 3
    depth = table.reshape(slabs, 2 * per_slab, extent)
    cosine, sine = np_phases(indices, indices, extent)
    across = np.block([[cosine, sine], [-sine, cosine]])
    high, low = np_split(across.T)
    across_back = np.concatenate([high, high, low], axis=1)
    high, low = np_split(across)
    along_back = np.concatenate([high, high, low], axis=0)
    return (
        jnp.asarray(depth, jnp.float32),
        jnp.asarray(across, jnp.float32),
        jnp.asarray(across_back),
        jnp.asarray(across.T, jnp.float32),
        jnp.asarray(along_back),
        jnp.asarray(backward, jnp.float32),
    )


def summed_density(columns, lines, weight, extent):
    _, rows, lanes = columns.shape
    bands = lines.shape[1] // (2 * extent)
    planes = extent // 4
    peers = lax.axis_size("band")
    share = extent // peers
    left, right = plane_tables(bands, extent)
    *tables, backward = line_tables(extent, 4, peers)
    per_slab = tables[0].shape[1] // 2
    each = per_slab // peers
    pieces = 8
    vmem = pl.BlockSpec(memory_space=pltpu.VMEM)
    density, final = pl.pallas_call(
        density_kernel,
        in_specs=[pl.BlockSpec(memory_space=pl.ANY)] + [vmem] * 9,
        out_specs=(vmem, vmem),
        out_shape=(
            jax.ShapeDtypeStruct((extent, share, extent), jnp.float32),
            jax.ShapeDtypeStruct((4, planes, 2 * per_slab * share), jnp.float32),
        ),
        scratch_shapes=[
            pltpu.VMEM((2, planes, rows, lanes), jnp.float32),
            pltpu.VMEM((planes, 8, lanes), jnp.float32),
            pltpu.VMEM((planes, lines.shape[1]), jnp.float32),
            pltpu.VMEM((planes, extent, extent), jnp.float32),
            pltpu.VMEM((peers - 1, planes, share, extent), jnp.float32),
            pltpu.SemaphoreType.DMA((3, pieces)),
            pltpu.SemaphoreType.DMA((2, pieces)),
            pltpu.SemaphoreType.DMA((3,)),
            pltpu.SemaphoreType.DMA((2,)),
            pltpu.SemaphoreType.DMA((2,)),
            pltpu.SemaphoreType.DMA((peers - 1, pieces)),
            pltpu.SemaphoreType.DMA((peers - 1, pieces)),
            pltpu.VMEM((extent, share, extent), jnp.float32),
            pltpu.VMEM((2, per_slab, share, extent), jnp.float32),
            pltpu.VMEM((2, each, extent, extent), jnp.float32),
            pltpu.VMEM((2, each, extent, extent), jnp.float32),
            pltpu.VMEM((2, per_slab, share, extent), jnp.float32),
            pltpu.VMEM((2, per_slab, share, extent), jnp.float32),
            pltpu.VMEM((extent, 2 * per_slab * share), jnp.float32),
            pltpu.VMEM((4, planes, 2 * per_slab * share), jnp.float32),
            pltpu.SemaphoreType.DMA((3, pieces)),
            pltpu.SemaphoreType.DMA((3, pieces)),
            pltpu.SemaphoreType.DMA((2, peers - 1)),
            pltpu.SemaphoreType.DMA((2, peers - 1)),
            pltpu.SemaphoreType.DMA((3,)),
            pltpu.SemaphoreType.DMA((3,)),
        ],
        compiler_params=pltpu.CompilerParams(
            vmem_limit_bytes=40 << 20, collective_id=0, has_side_effects=True
        ),
        cost_estimate=pl.CostEstimate(
            flops=2 * planes * extent * right.shape[0] * right.shape[1],
            bytes_accessed=4 * planes * (2 * rows * lanes + extent * extent),
            transcendentals=0,
        ),
    )(columns, lines, weight, left, right, *tables)
    final = final.reshape(4, planes, 2, per_slab, share)
    hartree = jnp.einsum("syckx,sckz->xyz", final, backward, precision=lax.Precision.HIGHEST)
    own = lax.dynamic_slice_in_dim(density, lax.axis_index("slab") * planes, planes, 2)
    return hartree, own.transpose(1, 2, 0)


def quartered(wave_coeffs, column_mask, occupations, core_density):
    bands, _, rows, extent = wave_coeffs.shape[:4]
    quarter = extent // 4
    slab_index = lax.axis_index("slab")
    mask_rows = lax.dynamic_slice_in_dim(column_mask, slab_index * rows, rows, 0).astype(jnp.float32)
    kept = jnp.concatenate([mask_rows[:, :quarter], mask_rows[:, 3 * quarter :]], axis=1)
    lane_mask = jnp.tile(kept, (1, 2 * bands))
    columns = transform_columns(wave_coeffs, lane_mask, extent)
    cosine_table, sine_table = dft_tables(extent)
    inside = jnp.where(slab_index == 0, column_mask[0, quarter], 0).astype(jnp.float32)
    single = wave_coeffs[:, :, 0, quarter] * inside
    single_real, single_imag = rotate(
        single[:, 0], single[:, 1], "bz,zw->bw", cosine_table, sine_table, 1.0
    )
    phase_real, phase_imag = cosine_table[quarter], sine_table[quarter]
    line_real = single_real[..., None] * phase_real - single_imag[..., None] * phase_imag
    line_imag = single_real[..., None] * phase_imag + single_imag[..., None] * phase_real
    lines = jnp.concatenate([line_real, line_imag], axis=2).transpose(1, 0, 2)
    lines = lines.reshape(extent, bands * 2 * extent)
    bands_all = lax.axis_size("band") * bands
    weight = jnp.repeat(occupations / (float(extent) ** 3 * bands_all), 2 * extent)[None]
    hartree, density = summed_density(columns, lines, weight, extent)
    xc_potential = exchange_correlation(density + core_density)
    return (hartree, xc_potential)


def solution(mesh):
    body = quartered if mesh.shape["slab"] == 4 else local
    return jax.shard_map(
        body,
        mesh=mesh,
        in_specs=(P("band", None, "slab", None, None), P(), P("band"), P("band", "slab", None)),
        out_specs=(P("band", "slab", None), P("band", "slab", None)),
        check_vma=False,
    )
```
